32 devices in a mesh: dp: 8 (over z, y), fsdp: 4 (over x, core).
Axes of the slice: x: 2, y: 2, z: 4, core: 2. Of those that a mesh axis runs over, the one named last changes fastest.
Arguments:
- features: bfloat16 [6144, 8192], P(('dp', 'fsdp')), may hold values from -6 to 6
- grad_out: bfloat16 [6144, 8192], P(('dp', 'fsdp')), may hold values from -6 to 6
- weight_tiles: bfloat16 [256, 128, 128], P('fsdp'), may hold values from -0.25 to 0.25
- tile_row: int32 [256], replicated, may hold values from 0 to 63, as said below
- tile_column: int32 [256], replicated, may hold values from 0 to 63, as said below
Outputs:
- grad_features: bfloat16 [6144, 8192], P(('dp', 'fsdp'))
- tile_update: float32 [256, 128, 128], P('fsdp')
The draws below stay inside these ranges and needn't reach their ends.
Inputs may be any that keep to these rules, and one draw needn't show every extreme that they name: `tile_row`: every tile-row holds exactly 4 stored tiles; the tile-columns of tile-row i are i XOR s for the four values s in (0, 2^a, 2^b, 2^a + 2^b), with two distinct bits a, b drawn per run; the stored order is a random permutation of the pattern. Every tile-column holds exactly 4 stored tiles; no (tile_row, tile_column) pair appears twice.
All inputs are finite; a program needn't handle non-finite values.
Results may differ from the reference program's by a relative error of at most 0.0034.
Values may be sent and summed in bfloat16 or wider, within the bound.
A program may use at most 128 MiB of HBM per device.

```python
import math
import jax
import jax.numpy as jnp
from jax import lax

WIDTH = 8192
TILE = 128
PER_ROW = 4
ROWS_DEV = 192
BLOCKS = 64
NTILES = 256
ROWS = 6144
N_DP = 8
N_FSDP = 4


def butterfly(key):
    blocks = WIDTH // TILE
    levels = blocks.bit_length() - 1
    chosen = jax.random.permutation(jax.random.fold_in(key, 7), levels)[:2].astype(jnp.int32)
    first_bit = jnp.left_shift(jnp.int32(1), chosen[0])
    second_bit = jnp.left_shift(jnp.int32(1), chosen[1])
    masks = jnp.stack([jnp.int32(0) * first_bit, first_bit, second_bit, first_bit + second_bit]).astype(jnp.int32)
    row_list = jnp.repeat(jnp.arange(blocks, dtype=jnp.int32), PER_ROW)
    column_list = jnp.bitwise_xor(row_list, jnp.tile(masks, blocks))
    shuffle = jax.random.permutation(jax.random.fold_in(key, 11), NTILES)
    return (row_list[shuffle].astype(jnp.int32), column_list[shuffle].astype(jnp.int32))


def draw_tile_row(key, part):
    return butterfly(key)[0]


def draw_tile_column(key, part):
    return butterfly(key)[1]


def shard_levels(key, dims, split, low, high):
    def one(position, blocks):
        draws = jax.random.uniform(jax.random.fold_in(jax.random.fold_in(key, 6), position), (blocks,), jnp.float32, low / len(split), high / len(split))
        return jnp.repeat(jnp.exp(draws), dims[position] // blocks).reshape((-1,) + (1,) * (len(dims) - position - 1))

    factor_of = one(*split[0])
    for cut in split[1:]:
        factor_of = factor_of * one(*cut)
    return factor_of


def scatter_about(stream_key, extent, deviation, bound, shards=(), held_as=jnp.bfloat16):
    level = shard_levels(stream_key, extent, shards, -0.22, 0.18) if shards else 1.0
    values = jax.random.normal(stream_key, extent, jnp.float32) * deviation * level
    return jnp.minimum(jnp.maximum(values, -bound), bound).astype(held_as)


def setup_inputs(seed: int = 0) -> dict:
    key_of = jax.random.split(jax.random.key(seed), 6)
    features = scatter_about(key_of[0], (ROWS, WIDTH), 1.0, 6.0, ((0, 32),))
    grad_out = scatter_about(key_of[1], (ROWS, WIDTH), 1.0, 6.0, ((0, 32),))
    weight_tiles = scatter_about(key_of[2], (NTILES, TILE, TILE), (PER_ROW * TILE) ** -0.5, 0.25, ((0, 4),))
    tile_row = draw_tile_row(jax.random.fold_in(key_of[5], 71), 0)
    tile_column = draw_tile_column(jax.random.fold_in(key_of[5], 71), 0)
    return {"features": features, "grad_out": grad_out, "weight_tiles": weight_tiles, "tile_row": tile_row, "tile_column": tile_column}


def gelu_slope(value):
    root_term = math.sqrt(2.0 / math.pi)
    inner = root_term * (value + 0.044715 * value * value * value)
    hyper = jnp.tanh(inner)
    return 0.5 * (1.0 + hyper) + 0.5 * value * (1.0 - hyper * hyper) * root_term * (1.0 + 3.0 * 0.044715 * value * value)

def reference(features, grad_out, weight_tiles, tile_row, tile_column):
    devices_all = N_DP * N_FSDP
    ordering = jnp.argsort(tile_row, stable=True)
    sorted_columns = tile_column[ordering].reshape(BLOCKS, PER_ROW)
    sorted_tiles = weight_tiles[ordering].astype(jnp.float32).reshape(BLOCKS, PER_ROW, TILE, TILE)
    feature_dev = features.reshape(devices_all, ROWS_DEV, BLOCKS, TILE)
    grad_dev = grad_out.reshape(devices_all, ROWS_DEV, BLOCKS, TILE)

    def per_device(total, inputs):
        feature_blocks, grad_blocks = inputs
        gathered = feature_blocks[:, sorted_columns].astype(jnp.float32)
        preact = jnp.einsum('rnkc,nkcd->rnd', gathered, sorted_tiles)
        slope_grad = (grad_blocks.astype(jnp.float32) * gelu_slope(preact)).astype(jnp.bfloat16)
        returned = jnp.einsum('rnd,nkcd->rnkc', slope_grad.astype(jnp.float32), sorted_tiles)
        spread = jnp.zeros((ROWS_DEV, BLOCKS, TILE), jnp.float32).at[:, sorted_columns].add(returned)
        grad_rows = (grad_blocks.astype(jnp.float32) + spread).astype(jnp.bfloat16)
        partial_value = jnp.einsum('rtc,rtd->tcd', feature_blocks[:, tile_column].astype(jnp.float32), slope_grad[:, tile_row].astype(jnp.float32))
        return (total + partial_value, grad_rows)
    weight_grad, grad_rows = lax.scan(per_device, jnp.zeros((NTILES, TILE, TILE), jnp.float32), (feature_dev, grad_dev))
    grad_features = grad_rows.reshape(ROWS, WIDTH)
    tile_update = weight_grad * lax.rsqrt(lax.optimization_barrier(jnp.mean(weight_grad * weight_grad, axis=(1, 2), keepdims=True)) + 1e-06)
    return (grad_features, tile_update)
```

```python
import functools
import math

import jax
import jax.numpy as jnp
from jax import lax
from jax.experimental import pallas as pl
from jax.experimental.pallas import tpu as pltpu
from jax.sharding import PartitionSpec as P

SIDE_BLOCKS = 4
ROOT = math.sqrt(2.0 / math.pi)


def gelu_slope(value):
    square = value * value
    hyper = jnp.tanh(ROOT * (value + 0.044715 * square * value))
    return 0.5 * (1.0 + hyper) + 0.5 * value * (1.0 - hyper * hyper) * ROOT * (
        1.0 + 3.0 * 0.044715 * square
    )


def pattern(tile_row, tile_column, nblocks):
    total = tile_row.shape[0]
    mask = jnp.max(jnp.bitwise_xor(tile_row, tile_column))
    ids = jnp.arange(nblocks, dtype=jnp.int32)
    keys = jnp.bitwise_and(ids, ~mask) * nblocks + jnp.bitwise_and(ids, mask)

    def place(block):
        key = jnp.bitwise_and(block, ~mask) * nblocks + jnp.bitwise_and(block, mask)
        return jnp.sum((keys[None, :] < key[:, None]).astype(jnp.int32), axis=1)

    places = place(ids)
    blocks = jnp.sum(jnp.where(places[None, :] == ids[:, None], ids[None, :], 0), axis=1)
    at_row, at_column = place(tile_row), place(tile_column)
    slots = at_column * SIDE_BLOCKS + at_row % SIDE_BLOCKS
    every = jnp.arange(total, dtype=jnp.int32)
    tiles = jnp.sum(jnp.where(slots[None, :] == every[:, None], every[None, :], 0), axis=1)
    return blocks, tiles


def layer_kernel(steps, blocks, tiles, places, *refs):
    n, m = SIDE_BLOCKS, SIDE_BLOCKS * SIDE_BLOCKS
    feature_refs, grad_refs, tile_refs = refs[:n], refs[n : 2 * n], refs[2 * n : 2 * n + m]
    out_ref, partial_ref, out_buf, partial_buf, sems = refs[2 * n + m :]
    side = tile_refs[0].shape[1]
    step = pl.program_id(0)
    slot = lax.rem(step, 2)

    def copies(at, to):
        found = []
        for k in range(n):
            column = pl.multiple_of(blocks[at * n + k] * side, side)
            found.append(
                pltpu.make_async_copy(
                    out_buf.at[to, k], out_ref.at[:, pl.ds(column, side)], sems.at[to, k]
                )
            )
        for k in range(m):
            found.append(
                pltpu.make_async_copy(
                    partial_buf.at[to, k], partial_ref.at[places[at * m + k]], sems.at[to, n + k]
                )
            )
        return found

    @pl.when(step >= 2)
    def _():
        for copy in copies(step - 2, slot):
            copy.wait()

    feature = jnp.concatenate([ref[...] for ref in feature_refs], axis=1)
    grad = jnp.concatenate([ref[...] for ref in grad_refs], axis=1).astype(jnp.float32)
    weight = jnp.concatenate(
        [
            jnp.concatenate([tile_refs[c * n + r][0] for r in range(n)], axis=1)
            for c in range(n)
        ],
        axis=0,
    )
    preact = jnp.dot(feature, weight, preferred_element_type=jnp.float32)
    slope = (grad * gelu_slope(preact)).astype(jnp.bfloat16)
    back = lax.dot_general(
        slope, weight, (((1,), (1,)), ((), ())), preferred_element_type=jnp.float32
    )
    result = (grad + back).astype(jnp.bfloat16)
    term = lax.dot_general(
        feature, slope, (((0,), (0,)), ((), ())), preferred_element_type=jnp.float32
    ).astype(jnp.bfloat16)
    for k in range(n):
        out_buf[slot, k] = result[:, k * side : (k + 1) * side]
    for c in range(n):
        for r in range(n):
            partial_buf[slot, c * n + r] = term[
                c * side : (c + 1) * side, r * side : (r + 1) * side
            ]
    for copy in copies(step, slot):
        copy.start()

    @pl.when(step == steps - 1)
    def _():
        if steps > 1:
            for copy in copies(step - 1, 1 - slot):
                copy.wait()
        for copy in copies(step, slot):
            copy.wait()


def layer(features, grad_out, whole, blocks, tiles, places):
    rows, width = features.shape
    total, side, _ = whole.shape
    n, m = SIDE_BLOCKS, SIDE_BLOCKS * SIDE_BLOCKS
    steps = width // side // n

    def column(k):
        return pl.BlockSpec((rows, side), lambda g, b, t, p: (0, b[g * n + k]))

    def tile(k):
        return pl.BlockSpec((1, side, side), lambda g, b, t, p: (t[g * m + k], 0, 0))

    return pl.pallas_call(
        functools.partial(layer_kernel, steps),
        grid_spec=pltpu.PrefetchScalarGridSpec(
            num_scalar_prefetch=3,
            grid=(steps,),
            in_specs=[column(k) for k in range(n)] * 2 + [tile(k) for k in range(m)],
            out_specs=[pl.BlockSpec(memory_space=pl.ANY)] * 2,
            scratch_shapes=[
                pltpu.VMEM((2, n, rows, side), jnp.bfloat16),
                pltpu.VMEM((2, m, side, side), jnp.bfloat16),
                pltpu.SemaphoreType.DMA((2, n + m)),
            ],
        ),
        out_shape=[
            jax.ShapeDtypeStruct((rows, width), jnp.bfloat16),
            jax.ShapeDtypeStruct((total, side, side), jnp.bfloat16),
        ],
        compiler_params=pltpu.CompilerParams(
            dimension_semantics=("arbitrary",), vmem_limit_bytes=32 * 2**20
        ),
        cost_estimate=pl.CostEstimate(
            flops=6 * rows * width * n * side,
            bytes_accessed=6 * rows * width + 4 * total * side * side,
            transcendentals=rows * width,
        ),
        name="layer",
    )(blocks, tiles, places, *[features] * n, *[grad_out] * n, *[whole] * m)


def on_device(features, grad_out, weight_tiles, tile_row, tile_column):
    side = weight_tiles.shape[1]
    nblocks = features.shape[1] // side
    blocks, tiles = pattern(tile_row, tile_column, nblocks)
    whole = lax.all_gather(weight_tiles, "fsdp", axis=0, tiled=True)
    grad_features, partial = layer(features, grad_out, whole, blocks, tiles, tiles)
    summed = lax.psum_scatter(partial, "fsdp", scatter_dimension=0, tiled=True)
    weight_grad = lax.psum(summed.astype(jnp.float32), "dp")
    tile_update = weight_grad * lax.rsqrt(
        jnp.mean(weight_grad * weight_grad, axis=(1, 2), keepdims=True) + 1e-06
    )
    return (grad_features, tile_update)


def solution(mesh):
    return jax.shard_map(
        on_device,
        mesh=mesh,
        in_specs=(
            P(("dp", "fsdp"), None),
            P(("dp", "fsdp"), None),
            P("fsdp", None, None),
            P(),
            P(),
        ),
        out_specs=(P(("dp", "fsdp"), None), P("fsdp", None, None)),
        check_vma=False,
    )
```

```python
import functools
import math

import jax
import jax.numpy as jnp
from jax import lax
from jax.experimental import pallas as pl
from jax.experimental.pallas import tpu as pltpu
from jax.sharding import PartitionSpec as P

SIDE_BLOCKS = 4
MESH = pl.DeviceIdType.MESH
ROOT = math.sqrt(2.0 / math.pi)


def gelu_slope(value):
    square = value * value
    hyper = jnp.tanh(ROOT * (value + 0.044715 * square * value))
    return 0.5 * (1.0 + hyper) + 0.5 * value * (1.0 - hyper * hyper) * ROOT * (
        1.0 + 3.0 * 0.044715 * square
    )


def pattern(tile_row, tile_column, nblocks):
    total = tile_row.shape[0]
    mask = jnp.max(jnp.bitwise_xor(tile_row, tile_column))
    ids = jnp.arange(nblocks, dtype=jnp.int32)
    keys = jnp.bitwise_and(ids, ~mask) * nblocks + jnp.bitwise_and(ids, mask)

    def place(block):
        key = jnp.bitwise_and(block, ~mask) * nblocks + jnp.bitwise_and(block, mask)
        return jnp.sum((keys[None, :] < key[:, None]).astype(jnp.int32), axis=1)

    places = place(ids)
    blocks = jnp.sum(jnp.where(places[None, :] == ids[:, None], ids[None, :], 0), axis=1)
    at_row, at_column = place(tile_row), place(tile_column)
    slots = at_column * SIDE_BLOCKS + at_row % SIDE_BLOCKS
    every = jnp.arange(total, dtype=jnp.int32)
    tiles = jnp.sum(jnp.where(slots[None, :] == every[:, None], every[None, :], 0), axis=1)
    return blocks, tiles


def layer_kernel(steps, blocks, tiles, places, *refs):
    n, m = SIDE_BLOCKS, SIDE_BLOCKS * SIDE_BLOCKS
    feature_refs, grad_refs, tile_refs = refs[:n], refs[n : 2 * n], refs[2 * n : 2 * n + m]
    out_ref, partial_ref, out_buf, partial_buf, sems = refs[2 * n + m :]
    side = tile_refs[0].shape[1]
    step = pl.program_id(0)
    slot = lax.rem(step, 2)

    def copies(at, to):
        found = []
        for k in range(n):
            column = pl.multiple_of(blocks[at * n + k] * side, side)
            found.append(
                pltpu.make_async_copy(
                    out_buf.at[to, k], out_ref.at[:, pl.ds(column, side)], sems.at[to, k]
                )
            )
        for k in range(m):
            found.append(
                pltpu.make_async_copy(
                    partial_buf.at[to, k], partial_ref.at[places[at * m + k]], sems.at[to, n + k]
                )
            )
        return found

    @pl.when(step >= 2)
    def _():
        for copy in copies(step - 2, slot):
            copy.wait()

    feature = jnp.concatenate([ref[...] for ref in feature_refs], axis=1)
    grad = jnp.concatenate([ref[...] for ref in grad_refs], axis=1).astype(jnp.float32)
    weight = jnp.concatenate(
        [
            jnp.concatenate([tile_refs[c * n + r][0] for r in range(n)], axis=1)
            for c in range(n)
        ],
        axis=0,
    )
    preact = jnp.dot(feature, weight, preferred_element_type=jnp.float32)
    slope = (grad * gelu_slope(preact)).astype(jnp.bfloat16)
    back = lax.dot_general(
        slope, weight, (((1,), (1,)), ((), ())), preferred_element_type=jnp.float32
    )
    result = (grad + back).astype(jnp.bfloat16)
    term = lax.dot_general(
        feature, slope, (((0,), (0,)), ((), ())), preferred_element_type=jnp.float32
    ).astype(jnp.bfloat16)
    for k in range(n):
        out_buf[slot, k] = result[:, k * side : (k + 1) * side]
    for c in range(n):
        for r in range(n):
            partial_buf[slot, c * n + r] = term[
                c * side : (c + 1) * side, r * side : (r + 1) * side
            ]
    for copy in copies(step, slot):
        copy.start()

    @pl.when(step == steps - 1)
    def _():
        if steps > 1:
            for copy in copies(step - 1, 1 - slot):
                copy.wait()
        for copy in copies(step, slot):
            copy.wait()


def layer(features, grad_out, whole, blocks, tiles, places):
    rows, width = features.shape
    total, side, _ = whole.shape
    n, m = SIDE_BLOCKS, SIDE_BLOCKS * SIDE_BLOCKS
    steps = width // side // n

    def column(k):
        return pl.BlockSpec((rows, side), lambda g, b, t, p: (0, b[g * n + k]))

    def tile(k):
        return pl.BlockSpec((1, side, side), lambda g, b, t, p: (t[g * m + k], 0, 0))

    return pl.pallas_call(
        functools.partial(layer_kernel, steps),
        grid_spec=pltpu.PrefetchScalarGridSpec(
            num_scalar_prefetch=3,
            grid=(steps,),
            in_specs=[column(k) for k in range(n)] * 2 + [tile(k) for k in range(m)],
            out_specs=[pl.BlockSpec(memory_space=pl.ANY)] * 2,
            scratch_shapes=[
                pltpu.VMEM((2, n, rows, side), jnp.bfloat16),
                pltpu.VMEM((2, m, side, side), jnp.bfloat16),
                pltpu.SemaphoreType.DMA((2, n + m)),
            ],
        ),
        out_shape=[
            jax.ShapeDtypeStruct((rows, width), jnp.bfloat16),
            jax.ShapeDtypeStruct((total, side, side), jnp.bfloat16),
        ],
        compiler_params=pltpu.CompilerParams(
            dimension_semantics=("arbitrary",), vmem_limit_bytes=32 * 2**20
        ),
        cost_estimate=pl.CostEstimate(
            flops=6 * rows * width * n * side,
            bytes_accessed=6 * rows * width + 4 * total * side * side,
            transcendentals=rows * width,
        ),
        name="layer",
    )(blocks, tiles, places, *[features] * n, *[grad_out] * n, *[whole] * m)


class Place:
    def __init__(self, n_dp, n_fsdp):
        self.cores = 2
        self.nx = n_fsdp // 2
        self.ny = 2 if n_dp <= 8 else 4
        self.nz = n_dp // self.ny

    def locate(self):
        fsdp, dp = lax.axis_index("fsdp"), lax.axis_index("dp")
        self.x, self.c = fsdp // 2, fsdp % 2
        self.z, self.y = dp // self.ny, dp % self.ny
        return self

    def at(self, x=None, c=None, y=None, z=None):
        x = self.x if x is None else x
        c = self.c if c is None else c
        y = self.y if y is None else y
        z = self.z if z is None else z
        return (z * self.ny + y, x * 2 + c)

    def step_x(self, k):
        return lax.rem(self.x + k + self.nx, self.nx)

    def step_y(self, k):
        return lax.rem(self.y + k + self.ny, self.ny)

    def step_z(self, k):
        return lax.rem(self.z + k + self.nz, self.nz)

    def x_peers(self):
        return [self.at(x=self.step_x(k)) for k in range(1, self.nx)]

    def y_peers(self):
        return [self.at(y=self.step_y(k)) for k in range(1, self.ny)]

    def z_peers(self):
        return [self.at(z=self.step_z(k)) for k in range(1, self.nz)]


def meet(peers):
    barrier = pltpu.get_barrier_semaphore()
    for peer in peers:
        pl.semaphore_signal(barrier, inc=1, device_id=peer, device_id_type=MESH)
    pl.semaphore_wait(barrier, len(peers))


def remote(src, dst, send, recv, peer):
    return pltpu.make_async_remote_copy(
        src_ref=src, dst_ref=dst, send_sem=send, recv_sem=recv, device_id=peer, device_id_type=MESH
    )


def gather_kernel(
    place, pieces, mine, whole, own_sem, xs, xr, ys, yr, cs, cr, ws, wr
):
    me = place.locate()
    tiles = mine.shape[0]
    part = tiles // me.ny
    q = part // pieces
    other = me.at(c=1 - me.c)
    xp, yp = me.x_peers(), me.y_peers()
    meet(xp + yp + [other])

    def span(x, y, p):
        return pl.ds((x * 2 + me.c) * tiles + y * part + p * q, q)

    started = []

    def go(copy):
        copy.start()
        started.append(copy)

    for p in range(pieces):
        for k in range(1, me.nx):
            go(
                remote(
                    mine.at[pl.ds(me.y * part + p * q, q)],
                    whole.at[span(me.x, me.y, p)],
                    xs.at[k - 1, p],
                    xr.at[k - 1, p],
                    xp[k - 1],
                )
            )
    home = pl.ds((me.x * 2 + me.c) * tiles, tiles)
    go(remote(mine, whole.at[home], ws, wr, other))
    local = pltpu.make_async_copy(mine, whole.at[home], own_sem)
    local.start()

    def to_other(x, y, k, j, p):
        at = whole.at[span(x, y, p)]
        go(remote(at, at, cs.at[k - 1, j, p], cr.at[k - 1, j, p], other))

    for p in range(pieces):
        for k in range(1, me.nx):
            x = me.step_x(-k)
            at = whole.at[span(x, me.y, p)]
            remote(at, at, xs.at[k - 1, p], xr.at[k - 1, p], xp[k - 1]).wait_recv()
            for j in range(1, me.ny):
                go(remote(at, at, ys.at[k - 1, j - 1, p], yr.at[k - 1, j - 1, p], yp[j - 1]))
            to_other(x, me.y, k, 0, p)
    for p in range(pieces):
        for k in range(1, me.nx):
            x = me.step_x(-k)
            for j in range(1, me.ny):
                y = me.step_y(-j)
                at = whole.at[span(x, y, p)]
                remote(
                    at, at, ys.at[k - 1, j - 1, p], yr.at[k - 1, j - 1, p], yp[j - 1]
                ).wait_recv()
                to_other(x, y, k, j, p)
    local.wait()
    away = whole.at[pl.ds((me.x * 2 + 1 - me.c) * tiles, tiles)]
    remote(away, away, ws, wr, other).wait_recv()
    for p in range(pieces):
        for k in range(1, me.nx):
            x = me.step_x(-k)
            for j in range(me.ny):
                y = me.step_y(-j)
                at = whole.at[
                    pl.ds((x * 2 + 1 - me.c) * tiles + y * part + p * q, q)
                ]
                remote(at, at, cs.at[k - 1, j, p], cr.at[k - 1, j, p], other).wait_recv()
    for copy in started:
        copy.wait_send()


def gather_tiles(mine, place):
    tiles, side, _ = mine.shape
    part = tiles // place.ny
    pieces = 4 if part % 4 == 0 else 1
    nx, ny = place.nx, place.ny
    dma = pltpu.SemaphoreType.DMA
    return pl.pallas_call(
        functools.partial(gather_kernel, place, pieces),
        in_specs=[pl.BlockSpec(memory_space=pl.ANY)],
        out_specs=pl.BlockSpec(memory_space=pl.ANY),
        out_shape=jax.ShapeDtypeStruct((tiles * nx * 2, side, side), mine.dtype),
        scratch_shapes=[
            dma,
            dma((nx - 1, pieces)),
            dma((nx - 1, pieces)),
            dma((nx - 1, ny - 1, pieces)),
            dma((nx - 1, ny - 1, pieces)),
            dma((nx - 1, ny, pieces)),
            dma((nx - 1, ny, pieces)),
            dma,
            dma,
        ],
        compiler_params=pltpu.CompilerParams(collective_id=1, has_side_effects=True),
        name="gather_tiles",
    )(mine)


def reduce_kernel(
    place,
    pieces,
    q,
    terms,
    out,
    own,
    rc,
    sx,
    rx,
    sy,
    ry,
    sz,
    rz,
    done,
    own_sem,
    cs,
    cr,
    xs,
    xr,
    ys,
    yr,
    zs,
    zr,
    keep_sem,
    azs,
    azr,
    ays,
    ayr,
):
    me = place.locate()
    nx, ny, nz = me.nx, me.ny, me.nz
    other = me.at(c=1 - me.c)
    xp, yp, zp = me.x_peers(), me.y_peers(), me.z_peers()
    meet([other] + xp + yp + zp)
    started = []

    def go(copy):
        copy.start()
        started.append(copy)

    def wide(ref):
        return ref[...].astype(jnp.float32)

    def core_copy(p):
        return remote(terms.at[1 - me.c, p], rc.at[p], cs.at[p], cr.at[p], other)

    def own_copy(p):
        return pltpu.make_async_copy(terms.at[me.c, p], own.at[p], own_sem.at[p])

    def x_copy(p, k):
        return remote(sx.at[p, k - 1], rx.at[p, k - 1], xs.at[p, k - 1], xr.at[p, k - 1], xp[k - 1])

    def y_copy(p, j):
        return remote(sy.at[p, j - 1], ry.at[p, j - 1], ys.at[p, j - 1], yr.at[p, j - 1], yp[j - 1])

    def z_copy(p, m):
        return remote(sz.at[p, m - 1], rz.at[p, m - 1], zs.at[p, m - 1], zr.at[p, m - 1], zp[m - 1])

    def spread_z(p, m, z):
        return remote(
            done.at[p], out.at[p, me.y, z], azs.at[p, m - 1], azr.at[p, m - 1], zp[m - 1]
        )

    def spread_y(p, j, m, src, y, z):
        return remote(
            src, out.at[p, y, z], ays.at[p, j - 1, m], ayr.at[p, j - 1, m], yp[j - 1]
        )

    def keep_copy(p):
        return pltpu.make_async_copy(done.at[p], out.at[p, me.y, me.z], keep_sem.at[p])

    def over_x(p):
        own_copy(p).wait()
        core_copy(p).wait_recv()
        for k in range(1, nx):
            x = me.step_x(k)

            def body(n, carry):
                total = wide(own.at[p, x, n]) + wide(rc.at[p, x, n])
                sx[p, k - 1, n] = total.astype(jnp.bfloat16)
                return carry

            lax.fori_loop(0, ny * nz * q, body, 0)
            go(x_copy(p, k))

    def up_to_x(p, n):
        total = wide(own.at[p, me.x, n]) + wide(rc.at[p, me.x, n])
        for k in range(1, nx):
            total = total + wide(rx.at[p, k - 1, n])
        return total

    def up_to_y(p, n):
        total = up_to_x(p, me.y * (nz * q) + n)
        for j in range(1, ny):
            total = total + wide(ry.at[p, j - 1, n])
        return total

    def over_y(p):
        for k in range(1, nx):
            x_copy(p, k).wait_recv()
        for j in range(1, ny):
            first = me.step_y(j) * (nz * q)

            def body(n, carry):
                sy[p, j - 1, n] = up_to_x(p, first + n).astype(jnp.bfloat16)
                return carry

            lax.fori_loop(0, nz * q, body, 0)
            go(y_copy(p, j))

    def over_z(p):
        for j in range(1, ny):
            y_copy(p, j).wait_recv()
        for m in range(1, nz):
            first = me.step_z(m) * q

            def body(i, carry):
                sz[p, m - 1, i] = up_to_y(p, first + i).astype(jnp.bfloat16)
                return carry

            lax.fori_loop(0, q, body, 0)
            go(z_copy(p, m))

    def finish(p):
        for m in range(1, nz):
            z_copy(p, m).wait_recv()

        def body(i, carry):
            total = up_to_y(p, me.z * q + i)
            for m in range(1, nz):
                total = total + wide(rz.at[p, m - 1, i])
            scale = lax.rsqrt(jnp.mean(total * total, keepdims=True) + 1e-06)
            done[p, i] = (total * scale).astype(jnp.bfloat16)
            return carry

        lax.fori_loop(0, q, body, 0)
        for m in range(1, nz):
            go(spread_z(p, m, me.z))
        for j in range(1, ny):
            go(spread_y(p, j, 0, done.at[p], me.y, me.z))
        keep_copy(p).start()

    def pass_on(p):
        for m in range(1, nz):
            z = me.step_z(-m)
            spread_z(p, m, z).wait_recv()
            for j in range(1, ny):
                go(spread_y(p, j, m, out.at[p, me.y, z], me.y, z))

    def collect(p):
        for j in range(1, ny):
            y = me.step_y(-j)
            for m in range(nz):
                z = me.step_z(-m)
                spread_y(p, j, m, done.at[p], y, z).wait_recv()

    for p in range(pieces):
        go(core_copy(p))
        own_copy(p).start()
    stages = [over_x, over_y, over_z, finish, pass_on, collect]
    for t in range(pieces + len(stages) - 1):
        for s, stage in enumerate(stages):
            if 0 <= t - s < pieces:
                stage(t - s)
    for p in range(pieces):
        keep_copy(p).wait()
    for copy in started:
        copy.wait_send()


def reduce_terms(terms, place, pieces, q):
    side = terms.shape[-1]
    nx, ny, nz = place.nx, place.ny, place.nz
    n = ny * nz * q
    dma = pltpu.SemaphoreType.DMA

    def room(*lead):
        return pltpu.VMEM((pieces,) + lead + (side, side), jnp.bfloat16)

    return pl.pallas_call(
        functools.partial(reduce_kernel, place, pieces, q),
        in_specs=[pl.BlockSpec(memory_space=pl.ANY)],
        out_specs=pl.BlockSpec(memory_space=pl.ANY),
        out_shape=jax.ShapeDtypeStruct((pieces, ny, nz, q, side, side), jnp.bfloat16),
        scratch_shapes=[
            room(nx, n),
            room(nx, n),
            room(nx - 1, n),
            room(nx - 1, n),
            room(ny - 1, nz * q),
            room(ny - 1, nz * q),
            room(nz - 1, q),
            room(nz - 1, q),
            room(q),
            dma((pieces,)),
            dma((pieces,)),
            dma((pieces,)),
            dma((pieces, nx - 1)),
            dma((pieces, nx - 1)),
            dma((pieces, ny - 1)),
            dma((pieces, ny - 1)),
            dma((pieces, nz - 1)),
            dma((pieces, nz - 1)),
            dma((pieces,)),
            dma((pieces, nz - 1)),
            dma((pieces, nz - 1)),
            dma((pieces, ny - 1, nz)),
            dma((pieces, ny - 1, nz)),
        ],
        compiler_params=pltpu.CompilerParams(
            collective_id=2, has_side_effects=True, vmem_limit_bytes=40 * 2**20
        ),
        name="reduce_terms",
    )(terms)


def on_device(n_dp, n_fsdp, features, grad_out, weight_tiles, tile_row, tile_column):
    tiles_here, side, _ = weight_tiles.shape
    nblocks = features.shape[1] // side
    place = Place(n_dp, n_fsdp)
    nx, n = place.nx, place.ny * place.nz
    pieces = max(count for count in (1, 2, 4, 8) if tiles_here % (n * count) == 0)
    n = tiles_here // pieces
    blocks, tiles = pattern(tile_row, tile_column, nblocks)
    owner, rest = tiles // tiles_here, tiles % tiles_here
    places = ((owner % 2 * pieces + rest // n) * nx + owner // 2) * n + rest % n
    whole = gather_tiles(weight_tiles, place)
    grad_features, partial = layer(features, grad_out, whole, blocks, tiles, places)
    terms = partial.reshape(2, pieces, nx, n, side, side)
    tile_update = reduce_terms(terms, place, pieces, n // (place.ny * place.nz))
    return (grad_features, tile_update.reshape(tiles_here, side, side).astype(jnp.float32))


def solution(mesh):
    return jax.shard_map(
        functools.partial(on_device, mesh.shape["dp"], mesh.shape["fsdp"]),
        mesh=mesh,
        in_specs=(
            P(("dp", "fsdp"), None),
            P(("dp", "fsdp"), None),
            P("fsdp", None, None),
            P(),
            P(),
        ),
        out_specs=(P(("dp", "fsdp"), None), P("fsdp", None, None)),
        check_vma=False,
    )
```

```python
import functools
import math

import jax
import jax.numpy as jnp
from jax import lax
from jax.experimental import pallas as pl
from jax.experimental.pallas import tpu as pltpu
from jax.sharding import PartitionSpec as P

SIDE_BLOCKS = 4
MESH = pl.DeviceIdType.MESH
WINDOW = 3
ROOT = math.sqrt(2.0 / math.pi)


def gelu_slope(value):
    square = value * value
    hyper = jnp.tanh(ROOT * (value + 0.044715 * square * value))
    return 0.5 * (1.0 + hyper) + 0.5 * value * (1.0 - hyper * hyper) * ROOT * (
        1.0 + 3.0 * 0.044715 * square
    )


def pattern(tile_row, tile_column, nblocks):
    total = tile_row.shape[0]
    mask = jnp.max(jnp.bitwise_xor(tile_row, tile_column))
    ids = jnp.arange(nblocks, dtype=jnp.int32)
    keys = jnp.bitwise_and(ids, ~mask) * nblocks + jnp.bitwise_and(ids, mask)

    def place(block):
        key = jnp.bitwise_and(block, ~mask) * nblocks + jnp.bitwise_and(block, mask)
        return jnp.sum((keys[None, :] < key[:, None]).astype(jnp.int32), axis=1)

    places = place(ids)
    blocks = jnp.sum(jnp.where(places[None, :] == ids[:, None], ids[None, :], 0), axis=1)
    at_row, at_column = place(tile_row), place(tile_column)
    slots = at_column * SIDE_BLOCKS + at_row % SIDE_BLOCKS
    every = jnp.arange(total, dtype=jnp.int32)
    tiles = jnp.sum(jnp.where(slots[None, :] == every[:, None], every[None, :], 0), axis=1)
    return blocks, tiles


def layer_kernel(steps, blocks, tiles, places, features, grads, whole, out_ref, partial_ref, term_buf, sems):
    n, m = SIDE_BLOCKS, SIDE_BLOCKS * SIDE_BLOCKS
    side = whole.shape[1]

    def drain(slot):
        pltpu.make_async_copy(
            term_buf.at[slot], partial_ref.at[pl.ds(0, m)], sems.at[slot]
        ).wait()

    def group(g, slot):
        columns = [
            pl.ds(pl.multiple_of(blocks[g * n + k] * side, side), side) for k in range(n)
        ]
        feature = jnp.concatenate([features[:, at] for at in columns], axis=1)
        grad = jnp.concatenate([grads[:, at] for at in columns], axis=1).astype(jnp.float32)
        weight = jnp.concatenate(
            [
                jnp.concatenate([whole[tiles[g * m + c * n + r]] for r in range(n)], axis=1)
                for c in range(n)
            ],
            axis=0,
        )
        preact = jnp.dot(feature, weight, preferred_element_type=jnp.float32)
        slope = (grad * gelu_slope(preact)).astype(jnp.bfloat16)
        back = lax.dot_general(
            slope, weight, (((1,), (1,)), ((), ())), preferred_element_type=jnp.float32
        )
        result = (grad + back).astype(jnp.bfloat16)
        for k, at in enumerate(columns):
            out_ref[:, at] = result[:, k * side : (k + 1) * side]
        term = lax.dot_general(
            feature, slope, (((0,), (0,)), ((), ())), preferred_element_type=jnp.float32
        )
        for c in range(n):
            for r in range(n):
                term_buf[slot, c * n + r] = term[
                    c * side : (c + 1) * side, r * side : (r + 1) * side
                ]
        for k in range(m):
            pltpu.make_async_copy(
                term_buf.at[slot, k], partial_ref.at[places[g * m + k]], sems.at[slot]
            ).start()

    slots = term_buf.shape[0]

    def body(i, carry):
        for k in range(slots):

            @pl.when(i > 0)
            def _():
                drain(k)

            group(i * slots + k, k)
        return carry

    lax.fori_loop(0, steps // slots, body, 0)
    for k in range(slots):
        drain(k)


def layer(features, grad_out, whole, blocks, tiles, places):
    rows, width = features.shape
    total, side, _ = whole.shape
    n, m = SIDE_BLOCKS, SIDE_BLOCKS * SIDE_BLOCKS
    steps = width // side // n
    slots = 2 if steps % 2 == 0 else 1
    vmem = pl.BlockSpec(memory_space=pltpu.VMEM)
    smem = pl.BlockSpec(memory_space=pltpu.SMEM)
    return pl.pallas_call(
        functools.partial(layer_kernel, steps),
        in_specs=[smem] * 3 + [vmem] * 3,
        out_specs=[vmem, pl.BlockSpec(memory_space=pl.ANY)],
        scratch_shapes=[
            pltpu.VMEM((slots, m, side, side), jnp.float32),
            pltpu.SemaphoreType.DMA((slots,)),
        ],
        out_shape=[
            jax.ShapeDtypeStruct((rows, width), jnp.bfloat16),
            jax.ShapeDtypeStruct((total, side, side), jnp.float32),
        ],
        compiler_params=pltpu.CompilerParams(vmem_limit_bytes=26 * 2**20),
        cost_estimate=pl.CostEstimate(
            flops=6 * rows * width * n * side,
            bytes_accessed=6 * rows * width + 6 * total * side * side,
            transcendentals=rows * width,
        ),
        name="layer",
    )(blocks, tiles, places, features, grad_out, whole)


class Place:
    def __init__(self, n_dp, n_fsdp):
        self.cores = 2
        self.nx = n_fsdp // 2
        self.ny = 2 if n_dp <= 8 else 4
        self.nz = n_dp // self.ny

    def locate(self):
        fsdp, dp = lax.axis_index("fsdp"), lax.axis_index("dp")
        self.x, self.c = fsdp // 2, fsdp % 2
        self.z, self.y = dp // self.ny, dp % self.ny
        return self

    def at(self, x=None, c=None, y=None, z=None):
        x = self.x if x is None else x
        c = self.c if c is None else c
        y = self.y if y is None else y
        z = self.z if z is None else z
        return (z * self.ny + y, x * 2 + c)

    def step_x(self, k):
        return lax.rem(self.x + k + self.nx, self.nx)

    def step_y(self, k):
        return lax.rem(self.y + k + self.ny, self.ny)

    def step_z(self, k):
        return lax.rem(self.z + k + self.nz, self.nz)

    def x_peers(self):
        return [self.at(x=self.step_x(k)) for k in range(1, self.nx)]

    def y_peers(self):
        return [self.at(y=self.step_y(k)) for k in range(1, self.ny)]

    def z_peers(self):
        return [self.at(z=self.step_z(k)) for k in range(1, self.nz)]


def meet(peers):
    barrier = pltpu.get_barrier_semaphore()
    for peer in peers:
        pl.semaphore_signal(barrier, inc=1, device_id=peer, device_id_type=MESH)
    pl.semaphore_wait(barrier, len(peers))


def remote(src, dst, send, recv, peer):
    return pltpu.make_async_remote_copy(
        src_ref=src, dst_ref=dst, send_sem=send, recv_sem=recv, device_id=peer, device_id_type=MESH
    )


def gather_kernel(
    place, pieces, mine, whole, own_sem, xs, xr, ys, yr, cs, cr, ws, wr
):
    me = place.locate()
    tiles = mine.shape[0]
    part = tiles // me.ny
    q = part // pieces
    other = me.at(c=1 - me.c)
    xp, yp = me.x_peers(), me.y_peers()
    meet(xp + yp + [other])

    def span(x, y, p):
        return pl.ds((x * 2 + me.c) * tiles + y * part + p * q, q)

    started = []

    def go(copy):
        copy.start()
        started.append(copy)

    def x_copy(p, k):
        return remote(
            mine.at[pl.ds(me.y * part + p * q, q)],
            whole.at[span(me.x, me.y, p)],
            xs.at[k - 1, p],
            xr.at[k - 1, p],
            xp[k - 1],
        )

    def home(core, p):
        return pl.ds((me.x * 2 + core) * tiles + p * q * me.ny, q * me.ny)

    def own_copy(p):
        src = mine.at[pl.ds(p * q * me.ny, q * me.ny)]
        return pltpu.make_async_copy(src, whole.at[home(me.c, p)], own_sem.at[p])

    def core_copy(p):
        src = mine.at[pl.ds(p * q * me.ny, q * me.ny)]
        return remote(src, whole.at[home(me.c, p)], ws.at[p], wr.at[p], other)

    def to_other(x, y, k, j, p):
        at = whole.at[span(x, y, p)]
        go(remote(at, at, cs.at[k - 1, j, p], cr.at[k - 1, j, p], other))

    def y_copy(p, k, j, y):
        at = whole.at[span(me.step_x(-k), y, p)]
        return remote(at, at, ys.at[k - 1, j - 1, p], yr.at[k - 1, j - 1, p], yp[j - 1])

    def land_x(p):
        for k in range(1, me.nx):
            x = me.step_x(-k)
            x_copy(p, k).wait_send()
            remote(
                mine.at[pl.ds(0, q)], whole.at[span(x, me.y, p)], xs.at[k - 1, p], xr.at[k - 1, p], xp[k - 1]
            ).wait_recv()
            if p + WINDOW < pieces:
                x_copy(p + WINDOW, k).start()
            for j in range(1, me.ny):
                go(y_copy(p, k, j, me.y))
            to_other(x, me.y, k, 0, p)
        go(core_copy(p))
        own_copy(p).start()

    def land_y(p):
        for k in range(1, me.nx):
            x = me.step_x(-k)
            for j in range(1, me.ny):
                y = me.step_y(-j)
                y_copy(p, k, j, y).wait_recv()
                to_other(x, y, k, j, p)

    for p in range(min(WINDOW, pieces)):
        for k in range(1, me.nx):
            x_copy(p, k).start()
    for t in range(pieces + 1):
        if t < pieces:
            land_x(t)
        if t >= 1:
            land_y(t - 1)
    for p in range(pieces):
        own_copy(p).wait()
        away = whole.at[home(1 - me.c, p)]
        remote(away, away, ws.at[p], wr.at[p], other).wait_recv()
        for k in range(1, me.nx):
            x = me.step_x(-k)
            for j in range(me.ny):
                y = me.step_y(-j)
                at = whole.at[
                    pl.ds((x * 2 + 1 - me.c) * tiles + y * part + p * q, q)
                ]
                remote(at, at, cs.at[k - 1, j, p], cr.at[k - 1, j, p], other).wait_recv()
    for copy in started:
        copy.wait_send()


def gather_tiles(mine, place):
    tiles, side, _ = mine.shape
    part = tiles // place.ny
    pieces = 8 if part % 8 == 0 else 1
    nx, ny = place.nx, place.ny
    dma = pltpu.SemaphoreType.DMA
    return pl.pallas_call(
        functools.partial(gather_kernel, place, pieces),
        in_specs=[pl.BlockSpec(memory_space=pl.ANY)],
        out_specs=pl.BlockSpec(memory_space=pl.ANY),
        out_shape=jax.ShapeDtypeStruct((tiles * nx * 2, side, side), mine.dtype),
        scratch_shapes=[
            dma((pieces,)),
            dma((nx - 1, pieces)),
            dma((nx - 1, pieces)),
            dma((nx - 1, ny - 1, pieces)),
            dma((nx - 1, ny - 1, pieces)),
            dma((nx - 1, ny, pieces)),
            dma((nx - 1, ny, pieces)),
            dma((pieces,)),
            dma((pieces,)),
        ],
        compiler_params=pltpu.CompilerParams(collective_id=1, has_side_effects=True),
        name="gather_tiles",
    )(mine)


def reduce_kernel(
    place,
    pieces,
    q,
    terms,
    out,
    own,
    rc,
    sx,
    rx,
    sy,
    ry,
    sz,
    rz,
    done,
    own_sem,
    cs,
    cr,
    xs,
    xr,
    ys,
    yr,
    zs,
    zr,
    keep_sem,
    azs,
    azr,
    ays,
    ayr,
):
    me = place.locate()
    nx, ny, nz = me.nx, me.ny, me.nz
    other = me.at(c=1 - me.c)
    xp, yp, zp = me.x_peers(), me.y_peers(), me.z_peers()
    meet([other] + xp + yp + zp)
    started = []

    def go(copy):
        copy.start()
        started.append(copy)

    def wide(ref):
        return ref[...].astype(jnp.float32)

    def core_copy(p):
        return remote(terms.at[1 - me.c, p], rc.at[p], cs.at[p], cr.at[p], other)

    def own_copy(p):
        return pltpu.make_async_copy(terms.at[me.c, p], own.at[p], own_sem.at[p])

    def x_copy(p, k):
        return remote(sx.at[p, k - 1], rx.at[p, k - 1], xs.at[p, k - 1], xr.at[p, k - 1], xp[k - 1])

    def y_copy(p, j):
        return remote(sy.at[p, j - 1], ry.at[p, j - 1], ys.at[p, j - 1], yr.at[p, j - 1], yp[j - 1])

    def z_copy(p, m):
        return remote(sz.at[p, m - 1], rz.at[p, m - 1], zs.at[p, m - 1], zr.at[p, m - 1], zp[m - 1])

    def spread_z(p, m, z):
        return remote(
            done.at[p], out.at[p, me.y, z], azs.at[p, m - 1], azr.at[p, m - 1], zp[m - 1]
        )

    def spread_y(p, j, m, src, y, z):
        return remote(
            src, out.at[p, y, z], ays.at[p, j - 1, m], ayr.at[p, j - 1, m], yp[j - 1]
        )

    def keep_copy(p):
        return pltpu.make_async_copy(done.at[p], out.at[p, me.y, me.z], keep_sem.at[p])

    def over_x(p):
        own_copy(p).wait()
        core_copy(p).wait_recv()
        if p + WINDOW < pieces:
            core_copy(p).wait_send()
            core_copy(p + WINDOW).start()
            own_copy(p + WINDOW).start()
        for k in range(1, nx):
            x = me.step_x(k)

            def body(n, carry):
                total = wide(own.at[p, x, n]) + wide(rc.at[p, x, n])
                sx[p, k - 1, n] = total.astype(jnp.bfloat16)
                return carry

            lax.fori_loop(0, ny * nz * q, body, 0)
            go(x_copy(p, k))

    def up_to_x(p, n):
        total = wide(own.at[p, me.x, n]) + wide(rc.at[p, me.x, n])
        for k in range(1, nx):
            total = total + wide(rx.at[p, k - 1, n])
        return total

    def up_to_y(p, n):
        total = up_to_x(p, me.y * (nz * q) + n)
        for j in range(1, ny):
            total = total + wide(ry.at[p, j - 1, n])
        return total

    def over_y(p):
        for k in range(1, nx):
            x_copy(p, k).wait_recv()
        for j in range(1, ny):
            first = me.step_y(j) * (nz * q)

            def body(n, carry):
                sy[p, j - 1, n] = up_to_x(p, first + n).astype(jnp.bfloat16)
                return carry

            lax.fori_loop(0, nz * q, body, 0)
            go(y_copy(p, j))

    def over_z(p):
        for j in range(1, ny):
            y_copy(p, j).wait_recv()
        for m in range(1, nz):
            first = me.step_z(m) * q

            def body(i, carry):
                sz[p, m - 1, i] = up_to_y(p, first + i).astype(jnp.bfloat16)
                return carry

            lax.fori_loop(0, q, body, 0)
            go(z_copy(p, m))

    def finish(p):
        for m in range(1, nz):
            z_copy(p, m).wait_recv()

        def body(i, carry):
            total = up_to_y(p, me.z * q + i)
            for m in range(1, nz):
                total = total + wide(rz.at[p, m - 1, i])
            scale = lax.rsqrt(jnp.mean(total * total, keepdims=True) + 1e-06)
            done[p, i] = (total * scale).astype(jnp.bfloat16)
            return carry

        lax.fori_loop(0, q, body, 0)
        for m in range(1, nz):
            go(spread_z(p, m, me.z))
        for j in range(1, ny):
            go(spread_y(p, j, 0, done.at[p], me.y, me.z))
        keep_copy(p).start()

    def pass_on(p):
        for m in range(1, nz):
            z = me.step_z(-m)
            spread_z(p, m, z).wait_recv()
            for j in range(1, ny):
                go(spread_y(p, j, m, out.at[p, me.y, z], me.y, z))

    def collect(p):
        for j in range(1, ny):
            y = me.step_y(-j)
            for m in range(nz):
                z = me.step_z(-m)
                spread_y(p, j, m, done.at[p], y, z).wait_recv()

    for p in range(min(WINDOW, pieces)):
        core_copy(p).start()
        own_copy(p).start()
    stages = [over_x, over_y, over_z, finish, pass_on, collect]
    for t in range(pieces + len(stages) - 1):
        for s, stage in enumerate(stages):
            if 0 <= t - s < pieces:
                stage(t - s)
    for p in range(pieces):
        keep_copy(p).wait()
        if p + WINDOW >= pieces:
            core_copy(p).wait_send()
    for copy in started:
        copy.wait_send()


def reduce_terms(terms, place, pieces, q):
    side = terms.shape[-1]
    nx, ny, nz = place.nx, place.ny, place.nz
    n = ny * nz * q
    dma = pltpu.SemaphoreType.DMA

    def room(*lead, dtype=jnp.bfloat16):
        return pltpu.VMEM((pieces,) + lead + (side, side), dtype)

    return pl.pallas_call(
        functools.partial(reduce_kernel, place, pieces, q),
        in_specs=[pl.BlockSpec(memory_space=pl.ANY)],
        out_specs=pl.BlockSpec(memory_space=pl.ANY),
        out_shape=jax.ShapeDtypeStruct((pieces, ny, nz, q, side, side), jnp.bfloat16),
        scratch_shapes=[
            room(nx, n, dtype=jnp.float32),
            room(nx, n, dtype=jnp.float32),
            room(nx - 1, n),
            room(nx - 1, n),
            room(ny - 1, nz * q),
            room(ny - 1, nz * q),
            room(nz - 1, q),
            room(nz - 1, q),
            room(q),
            dma((pieces,)),
            dma((pieces,)),
            dma((pieces,)),
            dma((pieces, nx - 1)),
            dma((pieces, nx - 1)),
            dma((pieces, ny - 1)),
            dma((pieces, ny - 1)),
            dma((pieces, nz - 1)),
            dma((pieces, nz - 1)),
            dma((pieces,)),
            dma((pieces, nz - 1)),
            dma((pieces, nz - 1)),
            dma((pieces, ny - 1, nz)),
            dma((pieces, ny - 1, nz)),
        ],
        compiler_params=pltpu.CompilerParams(
            collective_id=2, has_side_effects=True, vmem_limit_bytes=48 * 2**20
        ),
        name="reduce_terms",
    )(terms)


def on_device(n_dp, n_fsdp, features, grad_out, weight_tiles, tile_row, tile_column):
    tiles_here, side, _ = weight_tiles.shape
    nblocks = features.shape[1] // side
    place = Place(n_dp, n_fsdp)
    nx, n = place.nx, place.ny * place.nz
    pieces = max(count for count in (1, 2, 4, 8) if tiles_here % (n * count) == 0)
    n = tiles_here // pieces
    blocks, tiles = pattern(tile_row, tile_column, nblocks)
    owner, rest = tiles // tiles_here, tiles % tiles_here
    places = ((owner % 2 * pieces + rest // n) * nx + owner // 2) * n + rest % n
    whole = gather_tiles(weight_tiles, place)
    grad_features, partial = layer(features, grad_out, whole, blocks, tiles, places)
    terms = partial.reshape(2, pieces, nx, n, side, side)
    tile_update = reduce_terms(terms, place, pieces, n // (place.ny * place.nz))
    return (grad_features, tile_update.reshape(tiles_here, side, side).astype(jnp.float32))


def solution(mesh):
    return jax.shard_map(
        functools.partial(on_device, mesh.shape["dp"], mesh.shape["fsdp"]),
        mesh=mesh,
        in_specs=(
            P(("dp", "fsdp"), None),
            P(("dp", "fsdp"), None),
            P("fsdp", None, None),
            P(),
            P(),
        ),
        out_specs=(P(("dp", "fsdp"), None), P("fsdp", None, None)),
        check_vma=False,
    )
```

```python
import functools
import math

import jax
import jax.numpy as jnp
from jax import lax
from jax.experimental import pallas as pl
from jax.experimental.pallas import tpu as pltpu
from jax.sharding import PartitionSpec as P

SIDE_BLOCKS = 4
MESH = pl.DeviceIdType.MESH
WINDOW = 3
ROOT = math.sqrt(2.0 / math.pi)


def gelu_slope(value):
    square = value * value
    hyper = jnp.tanh(ROOT * (value + 0.044715 * square * value))
    return 0.5 * (1.0 + hyper) + 0.5 * value * (1.0 - hyper * hyper) * ROOT * (
        1.0 + 3.0 * 0.044715 * square
    )


def pattern(tile_row, tile_column, nblocks):
    total = tile_row.shape[0]
    mask = jnp.max(jnp.bitwise_xor(tile_row, tile_column))
    ids = jnp.arange(nblocks, dtype=jnp.int32)
    keys = jnp.bitwise_and(ids, ~mask) * nblocks + jnp.bitwise_and(ids, mask)

    def place(block):
        key = jnp.bitwise_and(block, ~mask) * nblocks + jnp.bitwise_and(block, mask)
        return jnp.sum((keys[None, :] < key[:, None]).astype(jnp.int32), axis=1)

    places = place(ids)
    blocks = jnp.sum(jnp.where(places[None, :] == ids[:, None], ids[None, :], 0), axis=1)
    at_row, at_column = place(tile_row), place(tile_column)
    slots = at_column * SIDE_BLOCKS + at_row % SIDE_BLOCKS
    every = jnp.arange(total, dtype=jnp.int32)
    tiles = jnp.sum(jnp.where(slots[None, :] == every[:, None], every[None, :], 0), axis=1)
    return blocks, tiles


def layer_kernel(steps, blocks, tiles, places, features, grads, whole, out_ref, partial_ref, term_buf, sems):
    n, m = SIDE_BLOCKS, SIDE_BLOCKS * SIDE_BLOCKS
    side = whole.shape[1]

    def drain(slot):
        pltpu.make_async_copy(
            term_buf.at[slot], partial_ref.at[pl.ds(0, m)], sems.at[slot]
        ).wait()

    def group(g, slot):
        columns = [
            pl.ds(pl.multiple_of(blocks[g * n + k] * side, side), side) for k in range(n)
        ]
        feature = jnp.concatenate([features[:, at] for at in columns], axis=1)
        grad = jnp.concatenate([grads[:, at] for at in columns], axis=1).astype(jnp.float32)
        weight = jnp.concatenate(
            [
                jnp.concatenate([whole[tiles[g * m + c * n + r]] for r in range(n)], axis=1)
                for c in range(n)
            ],
            axis=0,
        )
        preact = jnp.dot(feature, weight, preferred_element_type=jnp.float32)
        slope = (grad * gelu_slope(preact)).astype(jnp.bfloat16)
        back = lax.dot_general(
            slope, weight, (((1,), (1,)), ((), ())), preferred_element_type=jnp.float32
        )
        result = (grad + back).astype(jnp.bfloat16)
        for k, at in enumerate(columns):
            out_ref[:, at] = result[:, k * side : (k + 1) * side]
        term = lax.dot_general(
            feature, slope, (((0,), (0,)), ((), ())), preferred_element_type=jnp.float32
        )
        for c in range(n):
            for r in range(n):
                term_buf[slot, c * n + r] = term[
                    c * side : (c + 1) * side, r * side : (r + 1) * side
                ]
        for k in range(m):
            pltpu.make_async_copy(
                term_buf.at[slot, k], partial_ref.at[places[g * m + k]], sems.at[slot]
            ).start()

    slots = term_buf.shape[0]

    def body(i, carry):
        for k in range(slots):

            @pl.when(i > 0)
            def _():
                drain(k)

            group(i * slots + k, k)
        return carry

    lax.fori_loop(0, steps // slots, body, 0)
    for k in range(slots):
        drain(k)


def layer(features, grad_out, whole, blocks, tiles, places):
    rows, width = features.shape
    total, side, _ = whole.shape
    n, m = SIDE_BLOCKS, SIDE_BLOCKS * SIDE_BLOCKS
    steps = width // side // n
    slots = 2 if steps % 2 == 0 else 1
    vmem = pl.BlockSpec(memory_space=pltpu.VMEM)
    smem = pl.BlockSpec(memory_space=pltpu.SMEM)
    return pl.pallas_call(
        functools.partial(layer_kernel, steps),
        in_specs=[smem] * 3 + [vmem] * 3,
        out_specs=[vmem, pl.BlockSpec(memory_space=pl.ANY)],
        scratch_shapes=[
            pltpu.VMEM((slots, m, side, side), jnp.float32),
            pltpu.SemaphoreType.DMA((slots,)),
        ],
        out_shape=[
            jax.ShapeDtypeStruct((rows, width), jnp.bfloat16),
            jax.ShapeDtypeStruct((total, side, side), jnp.float32),
        ],
        compiler_params=pltpu.CompilerParams(vmem_limit_bytes=26 * 2**20),
        cost_estimate=pl.CostEstimate(
            flops=6 * rows * width * n * side,
            bytes_accessed=6 * rows * width + 6 * total * side * side,
            transcendentals=rows * width,
        ),
        name="layer",
    )(blocks, tiles, places, features, grad_out, whole)


class Place:
    def __init__(self, n_dp, n_fsdp):
        self.cores = 2
        self.nx = n_fsdp // 2
        self.ny = 2 if n_dp <= 8 else 4
        self.nz = n_dp // self.ny

    def locate(self):
        fsdp, dp = lax.axis_index("fsdp"), lax.axis_index("dp")
        self.x, self.c = fsdp // 2, fsdp % 2
        self.z, self.y = dp // self.ny, dp % self.ny
        return self

    def at(self, x=None, c=None, y=None, z=None):
        x = self.x if x is None else x
        c = self.c if c is None else c
        y = self.y if y is None else y
        z = self.z if z is None else z
        return (z * self.ny + y, x * 2 + c)

    def step_x(self, k):
        return lax.rem(self.x + k + self.nx, self.nx)

    def step_y(self, k):
        return lax.rem(self.y + k + self.ny, self.ny)

    def step_z(self, k):
        return lax.rem(self.z + k + self.nz, self.nz)

    def x_peers(self):
        return [self.at(x=self.step_x(k)) for k in range(1, self.nx)]

    def y_peers(self):
        return [self.at(y=self.step_y(k)) for k in range(1, self.ny)]

    def z_peers(self):
        return [self.at(z=self.step_z(k)) for k in range(1, self.nz)]


def meet(peers):
    barrier = pltpu.get_barrier_semaphore()
    for peer in peers:
        pl.semaphore_signal(barrier, inc=1, device_id=peer, device_id_type=MESH)
    pl.semaphore_wait(barrier, len(peers))


def remote(src, dst, send, recv, peer):
    return pltpu.make_async_remote_copy(
        src_ref=src, dst_ref=dst, send_sem=send, recv_sem=recv, device_id=peer, device_id_type=MESH
    )


def gather_kernel(
    place, pieces, mine, whole, own_sem, xs, xr, ys, yr, cs, cr, ws, wr
):
    me = place.locate()
    tiles = mine.shape[0]
    part = tiles // me.ny
    q = part // pieces
    other = me.at(c=1 - me.c)
    xp, yp = me.x_peers(), me.y_peers()
    meet(xp + yp + [other])

    def span(x, y, p):
        return pl.ds((x * 2 + me.c) * tiles + y * part + p * q, q)

    started = []

    def go(copy):
        copy.start()
        started.append(copy)

    def x_copy(p, k):
        return remote(
            mine.at[pl.ds(me.y * part + p * q, q)],
            whole.at[span(me.x, me.y, p)],
            xs.at[k - 1, p],
            xr.at[k - 1, p],
            xp[k - 1],
        )

    def home(core, p):
        return pl.ds((me.x * 2 + core) * tiles + p * q * me.ny, q * me.ny)

    def own_copy(p):
        src = mine.at[pl.ds(p * q * me.ny, q * me.ny)]
        return pltpu.make_async_copy(src, whole.at[home(me.c, p)], own_sem.at[p])

    def core_copy(p):
        src = mine.at[pl.ds(p * q * me.ny, q * me.ny)]
        return remote(src, whole.at[home(me.c, p)], ws.at[p], wr.at[p], other)

    def to_other(x, y, k, j, p):
        at = whole.at[span(x, y, p)]
        go(remote(at, at, cs.at[k - 1, j, p], cr.at[k - 1, j, p], other))

    def y_copy(p, k, j, y):
        at = whole.at[span(me.step_x(-k), y, p)]
        return remote(at, at, ys.at[k - 1, j - 1, p], yr.at[k - 1, j - 1, p], yp[j - 1])

    def land_x(p):
        for k in range(1, me.nx):
            x = me.step_x(-k)
            x_copy(p, k).wait_send()
            remote(
                mine.at[pl.ds(0, q)], whole.at[span(x, me.y, p)], xs.at[k - 1, p], xr.at[k - 1, p], xp[k - 1]
            ).wait_recv()
            if p + WINDOW < pieces:
                x_copy(p + WINDOW, k).start()
            for j in range(1, me.ny):
                go(y_copy(p, k, j, me.y))
            to_other(x, me.y, k, 0, p)
        go(core_copy(p))
        own_copy(p).start()

    def land_y(p):
        for k in range(1, me.nx):
            x = me.step_x(-k)
            for j in range(1, me.ny):
                y = me.step_y(-j)
                y_copy(p, k, j, y).wait_recv()
                to_other(x, y, k, j, p)

    for p in range(min(WINDOW, pieces)):
        for k in range(1, me.nx):
            x_copy(p, k).start()
    for t in range(pieces + 1):
        if t < pieces:
            land_x(t)
        if t >= 1:
            land_y(t - 1)
    for p in range(pieces):
        own_copy(p).wait()
        away = whole.at[home(1 - me.c, p)]
        remote(away, away, ws.at[p], wr.at[p], other).wait_recv()
        for k in range(1, me.nx):
            x = me.step_x(-k)
            for j in range(me.ny):
                y = me.step_y(-j)
                at = whole.at[
                    pl.ds((x * 2 + 1 - me.c) * tiles + y * part + p * q, q)
                ]
                remote(at, at, cs.at[k - 1, j, p], cr.at[k - 1, j, p], other).wait_recv()
    for copy in started:
        copy.wait_send()


def gather_tiles(mine, place):
    tiles, side, _ = mine.shape
    part = tiles // place.ny
    pieces = 8 if part % 8 == 0 else 1
    nx, ny = place.nx, place.ny
    dma = pltpu.SemaphoreType.DMA
    return pl.pallas_call(
        functools.partial(gather_kernel, place, pieces),
        in_specs=[pl.BlockSpec(memory_space=pltpu.VMEM)],
        out_specs=pl.BlockSpec(memory_space=pltpu.VMEM),
        out_shape=jax.ShapeDtypeStruct((tiles * nx * 2, side, side), mine.dtype),
        scratch_shapes=[
            dma((pieces,)),
            dma((nx - 1, pieces)),
            dma((nx - 1, pieces)),
            dma((nx - 1, ny - 1, pieces)),
            dma((nx - 1, ny - 1, pieces)),
            dma((nx - 1, ny, pieces)),
            dma((nx - 1, ny, pieces)),
            dma((pieces,)),
            dma((pieces,)),
        ],
        compiler_params=pltpu.CompilerParams(
            collective_id=1, has_side_effects=True, vmem_limit_bytes=24 * 2**20
        ),
        name="gather_tiles",
    )(mine)


def reduce_kernel(
    place,
    pieces,
    q,
    terms,
    out,
    own,
    rc,
    sx,
    rx,
    sy,
    ry,
    sz,
    rz,
    done,
    own_sem,
    cs,
    cr,
    xs,
    xr,
    ys,
    yr,
    zs,
    zr,
    keep_sem,
    azs,
    azr,
    ays,
    ayr,
):
    me = place.locate()
    nx, ny, nz = me.nx, me.ny, me.nz
    other = me.at(c=1 - me.c)
    xp, yp, zp = me.x_peers(), me.y_peers(), me.z_peers()
    meet([other] + xp + yp + zp)
    started = []

    def go(copy):
        copy.start()
        started.append(copy)

    def wide(ref):
        return ref[...].astype(jnp.float32)

    def core_copy(p):
        return remote(terms.at[1 - me.c, p], rc.at[p], cs.at[p], cr.at[p], other)

    def own_copy(p):
        return pltpu.make_async_copy(terms.at[me.c, p], own.at[p], own_sem.at[p])

    def x_copy(p, k):
        return remote(sx.at[p, k - 1], rx.at[p, k - 1], xs.at[p, k - 1], xr.at[p, k - 1], xp[k - 1])

    def y_copy(p, j):
        return remote(sy.at[p, j - 1], ry.at[p, j - 1], ys.at[p, j - 1], yr.at[p, j - 1], yp[j - 1])

    def z_copy(p, m):
        return remote(sz.at[p, m - 1], rz.at[p, m - 1], zs.at[p, m - 1], zr.at[p, m - 1], zp[m - 1])

    def spread_z(p, m, z):
        return remote(
            done.at[p], out.at[p, me.y, z], azs.at[p, m - 1], azr.at[p, m - 1], zp[m - 1]
        )

    def spread_y(p, j, m, src, y, z):
        return remote(
            src, out.at[p, y, z], ays.at[p, j - 1, m], ayr.at[p, j - 1, m], yp[j - 1]
        )

    def keep_copy(p):
        return pltpu.make_async_copy(done.at[p], out.at[p, me.y, me.z], keep_sem.at[p])

    def over_x(p):
        own_copy(p).wait()
        core_copy(p).wait_recv()
        if p + WINDOW < pieces:
            core_copy(p).wait_send()
            core_copy(p + WINDOW).start()
            own_copy(p + WINDOW).start()
        for k in range(1, nx):
            x = me.step_x(k)

            def body(n, carry):
                total = wide(own.at[p, x, n]) + wide(rc.at[p, x, n])
                sx[p, k - 1, n] = total.astype(jnp.bfloat16)
                return carry

            lax.fori_loop(0, ny * nz * q, body, 0)
            go(x_copy(p, k))

    def up_to_x(p, n):
        total = wide(own.at[p, me.x, n]) + wide(rc.at[p, me.x, n])
        for k in range(1, nx):
            total = total + wide(rx.at[p, k - 1, n])
        return total

    def up_to_y(p, n):
        total = up_to_x(p, me.y * (nz * q) + n)
        for j in range(1, ny):
            total = total + wide(ry.at[p, j - 1, n])
        return total

    def over_y(p):
        for k in range(1, nx):
            x_copy(p, k).wait_recv()
        for j in range(1, ny):
            first = me.step_y(j) * (nz * q)

            def body(n, carry):
                sy[p, j - 1, n] = up_to_x(p, first + n).astype(jnp.bfloat16)
                return carry

            lax.fori_loop(0, nz * q, body, 0)
            go(y_copy(p, j))

    def over_z(p):
        for j in range(1, ny):
            y_copy(p, j).wait_recv()
        for m in range(1, nz):
            first = me.step_z(m) * q

            def body(i, carry):
                sz[p, m - 1, i] = up_to_y(p, first + i).astype(jnp.bfloat16)
                return carry

            lax.fori_loop(0, q, body, 0)
            go(z_copy(p, m))

    def finish(p):
        for m in range(1, nz):
            z_copy(p, m).wait_recv()

        def body(i, carry):
            total = up_to_y(p, me.z * q + i)
            for m in range(1, nz):
                total = total + wide(rz.at[p, m - 1, i])
            scale = lax.rsqrt(jnp.mean(total * total, keepdims=True) + 1e-06)
            done[p, i] = (total * scale).astype(jnp.bfloat16)
            return carry

        lax.fori_loop(0, q, body, 0)
        for m in range(1, nz):
            go(spread_z(p, m, me.z))
        for j in range(1, ny):
            go(spread_y(p, j, 0, done.at[p], me.y, me.z))
        keep_copy(p).start()

    def pass_on(p):
        for m in range(1, nz):
            z = me.step_z(-m)
            spread_z(p, m, z).wait_recv()
            for j in range(1, ny):
                go(spread_y(p, j, m, out.at[p, me.y, z], me.y, z))

    def collect(p):
        for j in range(1, ny):
            y = me.step_y(-j)
            for m in range(nz):
                z = me.step_z(-m)
                spread_y(p, j, m, done.at[p], y, z).wait_recv()

    for p in range(min(WINDOW, pieces)):
        core_copy(p).start()
        own_copy(p).start()
    stages = [over_x, over_y, over_z, finish, pass_on, collect]
    for t in range(pieces + len(stages) - 1):
        for s, stage in enumerate(stages):
            if 0 <= t - s < pieces:
                stage(t - s)
    for p in range(pieces):
        keep_copy(p).wait()
        if p + WINDOW >= pieces:
            core_copy(p).wait_send()
    for copy in started:
        copy.wait_send()


def reduce_terms(terms, place, pieces, q):
    side = terms.shape[-1]
    nx, ny, nz = place.nx, place.ny, place.nz
    n = ny * nz * q
    dma = pltpu.SemaphoreType.DMA

    def room(*lead, dtype=jnp.bfloat16):
        return pltpu.VMEM((pieces,) + lead + (side, side), dtype)

    return pl.pallas_call(
        functools.partial(reduce_kernel, place, pieces, q),
        in_specs=[pl.BlockSpec(memory_space=pl.ANY)],
        out_specs=pl.BlockSpec(memory_space=pl.ANY),
        out_shape=jax.ShapeDtypeStruct((pieces, ny, nz, q, side, side), jnp.bfloat16),
        scratch_shapes=[
            room(nx, n, dtype=jnp.float32),
            room(nx, n, dtype=jnp.float32),
            room(nx - 1, n),
            room(nx - 1, n),
            room(ny - 1, nz * q),
            room(ny - 1, nz * q),
            room(nz - 1, q),
            room(nz - 1, q),
            room(q),
            dma((pieces,)),
            dma((pieces,)),
            dma((pieces,)),
            dma((pieces, nx - 1)),
            dma((pieces, nx - 1)),
            dma((pieces, ny - 1)),
            dma((pieces, ny - 1)),
            dma((pieces, nz - 1)),
            dma((pieces, nz - 1)),
            dma((pieces,)),
            dma((pieces, nz - 1)),
            dma((pieces, nz - 1)),
            dma((pieces, ny - 1, nz)),
            dma((pieces, ny - 1, nz)),
        ],
        compiler_params=pltpu.CompilerParams(
            collective_id=2, has_side_effects=True, vmem_limit_bytes=48 * 2**20
        ),
        name="reduce_terms",
    )(terms)


def on_device(n_dp, n_fsdp, features, grad_out, weight_tiles, tile_row, tile_column):
    tiles_here, side, _ = weight_tiles.shape
    nblocks = features.shape[1] // side
    place = Place(n_dp, n_fsdp)
    nx, n = place.nx, place.ny * place.nz
    pieces = max(count for count in (1, 2, 4, 8) if tiles_here % (n * count) == 0)
    n = tiles_here // pieces
    blocks, tiles = pattern(tile_row, tile_column, nblocks)
    owner, rest = tiles // tiles_here, tiles % tiles_here
    places = ((owner % 2 * pieces + rest // n) * nx + owner // 2) * n + rest % n
    whole = gather_tiles(weight_tiles, place)
    grad_features, partial = layer(features, grad_out, whole, blocks, tiles, places)
    terms = partial.reshape(2, pieces, nx, n, side, side)
    tile_update = reduce_terms(terms, place, pieces, n // (place.ny * place.nz))
    return (grad_features, tile_update.reshape(tiles_here, side, side).astype(jnp.float32))


def solution(mesh):
    return jax.shard_map(
        functools.partial(on_device, mesh.shape["dp"], mesh.shape["fsdp"]),
        mesh=mesh,
        in_specs=(
            P(("dp", "fsdp"), None),
            P(("dp", "fsdp"), None),
            P("fsdp", None, None),
            P(),
            P(),
        ),
        out_specs=(P(("dp", "fsdp"), None), P("fsdp", None, None)),
        check_vma=False,
    )
```

```python
import functools
import math

import jax
import jax.numpy as jnp
from jax import lax
from jax.experimental import pallas as pl
from jax.experimental.pallas import tpu as pltpu
from jax.sharding import PartitionSpec as P

SIDE_BLOCKS = 4
MESH = pl.DeviceIdType.MESH
WINDOW = 3
ROOT = math.sqrt(2.0 / math.pi)


def gelu_slope(value):
    square = value * value
    hyper = jnp.tanh(ROOT * (value + 0.044715 * square * value))
    return 0.5 * (1.0 + hyper) + 0.5 * value * (1.0 - hyper * hyper) * ROOT * (
        1.0 + 3.0 * 0.044715 * square
    )


def pattern(tile_row, tile_column, nblocks):
    total = tile_row.shape[0]
    mask = jnp.max(jnp.bitwise_xor(tile_row, tile_column))
    ids = jnp.arange(nblocks, dtype=jnp.int32)
    keys = jnp.bitwise_and(ids, ~mask) * nblocks + jnp.bitwise_and(ids, mask)

    def place(block):
        key = jnp.bitwise_and(block, ~mask) * nblocks + jnp.bitwise_and(block, mask)
        return jnp.sum((keys[None, :] < key[:, None]).astype(jnp.int32), axis=1)

    places = place(ids)
    blocks = jnp.sum(jnp.where(places[None, :] == ids[:, None], ids[None, :], 0), axis=1)
    at_row, at_column = place(tile_row), place(tile_column)
    slots = at_column * SIDE_BLOCKS + at_row % SIDE_BLOCKS
    every = jnp.arange(total, dtype=jnp.int32)
    tiles = jnp.sum(jnp.where(slots[None, :] == every[:, None], every[None, :], 0), axis=1)
    return blocks, tiles


def layer_kernel(steps, blocks, tiles, places, features, grads, whole, out_ref, partial_ref, term_buf, sems):
    n, m = SIDE_BLOCKS, SIDE_BLOCKS * SIDE_BLOCKS
    side = whole.shape[1]

    def drain(slot):
        pltpu.make_async_copy(
            term_buf.at[slot], partial_ref.at[pl.ds(0, m)], sems.at[slot]
        ).wait()

    def group(g, slot):
        columns = [
            pl.ds(pl.multiple_of(blocks[g * n + k] * side, side), side) for k in range(n)
        ]
        feature = jnp.concatenate([features[:, at] for at in columns], axis=1)
        grad = jnp.concatenate([grads[:, at] for at in columns], axis=1).astype(jnp.float32)
        weight = jnp.concatenate(
            [
                jnp.concatenate([whole[tiles[g * m + c * n + r]] for r in range(n)], axis=1)
                for c in range(n)
            ],
            axis=0,
        )
        preact = jnp.dot(feature, weight, preferred_element_type=jnp.float32)
        slope = (grad * gelu_slope(preact)).astype(jnp.bfloat16)
        back = lax.dot_general(
            slope, weight, (((1,), (1,)), ((), ())), preferred_element_type=jnp.float32
        )
        result = (grad + back).astype(jnp.bfloat16)
        for k, at in enumerate(columns):
            out_ref[:, at] = result[:, k * side : (k + 1) * side]
        term = lax.dot_general(
            feature, slope, (((0,), (0,)), ((), ())), preferred_element_type=jnp.float32
        )
        for c in range(n):
            for r in range(n):
                term_buf[slot, c * n + r] = term[
                    c * side : (c + 1) * side, r * side : (r + 1) * side
                ]
        for k in range(m):
            pltpu.make_async_copy(
                term_buf.at[slot, k], partial_ref.at[places[g * m + k]], sems.at[slot]
            ).start()

    slots = term_buf.shape[0]

    def body(i, carry):
        for k in range(slots):

            @pl.when(i > 0)
            def _():
                drain(k)

            group(i * slots + k, k)
        return carry

    lax.fori_loop(0, steps // slots, body, 0)
    for k in range(slots):
        drain(k)


def layer(features, grad_out, whole, blocks, tiles, places):
    rows, width = features.shape
    total, side, _ = whole.shape
    n, m = SIDE_BLOCKS, SIDE_BLOCKS * SIDE_BLOCKS
    steps = width // side // n
    slots = 2 if steps % 2 == 0 else 1
    vmem = pl.BlockSpec(memory_space=pltpu.VMEM)
    smem = pl.BlockSpec(memory_space=pltpu.SMEM)
    return pl.pallas_call(
        functools.partial(layer_kernel, steps),
        in_specs=[smem] * 3 + [vmem] * 3,
        out_specs=[vmem, pl.BlockSpec(memory_space=pl.ANY)],
        scratch_shapes=[
            pltpu.VMEM((slots, m, side, side), jnp.float32),
            pltpu.SemaphoreType.DMA((slots,)),
        ],
        out_shape=[
            jax.ShapeDtypeStruct((rows, width), jnp.bfloat16),
            jax.ShapeDtypeStruct((total, side, side), jnp.float32),
        ],
        compiler_params=pltpu.CompilerParams(vmem_limit_bytes=26 * 2**20),
        cost_estimate=pl.CostEstimate(
            flops=6 * rows * width * n * side,
            bytes_accessed=6 * rows * width + 6 * total * side * side,
            transcendentals=rows * width,
        ),
        name="layer",
    )(blocks, tiles, places, features, grad_out, whole)


class Place:
    def __init__(self, n_dp, n_fsdp):
        self.cores = 2
        self.nx = n_fsdp // 2
        self.ny = 2 if n_dp <= 8 else 4
        self.nz = n_dp // self.ny

    def locate(self):
        fsdp, dp = lax.axis_index("fsdp"), lax.axis_index("dp")
        self.x, self.c = fsdp // 2, fsdp % 2
        self.z, self.y = dp // self.ny, dp % self.ny
        return self

    def at(self, x=None, c=None, y=None, z=None):
        x = self.x if x is None else x
        c = self.c if c is None else c
        y = self.y if y is None else y
        z = self.z if z is None else z
        return (z * self.ny + y, x * 2 + c)

    def step_x(self, k):
        return lax.rem(self.x + k + self.nx, self.nx)

    def step_y(self, k):
        return lax.rem(self.y + k + self.ny, self.ny)

    def step_z(self, k):
        return lax.rem(self.z + k + self.nz, self.nz)

    def x_peers(self):
        return [self.at(x=self.step_x(k)) for k in range(1, self.nx)]

    def y_peers(self):
        return [self.at(y=self.step_y(k)) for k in range(1, self.ny)]

    def z_peers(self):
        return [self.at(z=self.step_z(k)) for k in range(1, self.nz)]


def meet(peers):
    barrier = pltpu.get_barrier_semaphore()
    for peer in peers:
        pl.semaphore_signal(barrier, inc=1, device_id=peer, device_id_type=MESH)
    pl.semaphore_wait(barrier, len(peers))


def remote(src, dst, send, recv, peer):
    return pltpu.make_async_remote_copy(
        src_ref=src, dst_ref=dst, send_sem=send, recv_sem=recv, device_id=peer, device_id_type=MESH
    )


def gather_kernel(
    place, pieces, mine, whole, own_sem, xs, xr, ys, yr, cs, cr, ws, wr
):
    me = place.locate()
    tiles = mine.shape[0]
    part = tiles // me.ny
    q = part // pieces
    other = me.at(c=1 - me.c)
    xp, yp = me.x_peers(), me.y_peers()
    meet(xp + yp + [other])

    def span(x, y, p):
        return pl.ds((x * 2 + me.c) * tiles + y * part + p * q, q)

    started = []

    def go(copy):
        copy.start()
        started.append(copy)

    def x_copy(p, k):
        return remote(
            mine.at[pl.ds(me.y * part + p * q, q)],
            whole.at[span(me.x, me.y, p)],
            xs.at[k - 1, p],
            xr.at[k - 1, p],
            xp[k - 1],
        )

    def home(core, p):
        return pl.ds((me.x * 2 + core) * tiles + p * q * me.ny, q * me.ny)

    def own_copy(p):
        src = mine.at[pl.ds(p * q * me.ny, q * me.ny)]
        return pltpu.make_async_copy(src, whole.at[home(me.c, p)], own_sem.at[p])

    def core_copy(p):
        src = mine.at[pl.ds(p * q * me.ny, q * me.ny)]
        return remote(src, whole.at[home(me.c, p)], ws.at[p], wr.at[p], other)

    def to_other(x, y, k, j, p):
        at = whole.at[span(x, y, p)]
        go(remote(at, at, cs.at[k - 1, j, p], cr.at[k - 1, j, p], other))

    def y_copy(p, k, j, y):
        at = whole.at[span(me.step_x(-k), y, p)]
        return remote(at, at, ys.at[k - 1, j - 1, p], yr.at[k - 1, j - 1, p], yp[j - 1])

    def land_x(p):
        for k in range(1, me.nx):
            x = me.step_x(-k)
            x_copy(p, k).wait_send()
            remote(
                mine.at[pl.ds(0, q)], whole.at[span(x, me.y, p)], xs.at[k - 1, p], xr.at[k - 1, p], xp[k - 1]
            ).wait_recv()
            if p + WINDOW < pieces:
                x_copy(p + WINDOW, k).start()
            for j in range(1, me.ny):
                go(y_copy(p, k, j, me.y))
            to_other(x, me.y, k, 0, p)
        go(core_copy(p))
        own_copy(p).start()

    def land_y(p):
        for k in range(1, me.nx):
            x = me.step_x(-k)
            for j in range(1, me.ny):
                y = me.step_y(-j)
                y_copy(p, k, j, y).wait_recv()
                to_other(x, y, k, j, p)

    for p in range(min(WINDOW, pieces)):
        for k in range(1, me.nx):
            x_copy(p, k).start()
    for t in range(pieces + 1):
        if t < pieces:
            land_x(t)
        if t >= 1:
            land_y(t - 1)
    for p in range(pieces):
        own_copy(p).wait()
        away = whole.at[home(1 - me.c, p)]
        remote(away, away, ws.at[p], wr.at[p], other).wait_recv()
        for k in range(1, me.nx):
            x = me.step_x(-k)
            for j in range(me.ny):
                y = me.step_y(-j)
                at = whole.at[
                    pl.ds((x * 2 + 1 - me.c) * tiles + y * part + p * q, q)
                ]
                remote(at, at, cs.at[k - 1, j, p], cr.at[k - 1, j, p], other).wait_recv()
    for copy in started:
        copy.wait_send()


def gather_tiles(mine, place):
    tiles, side, _ = mine.shape
    part = tiles // place.ny
    pieces = 8 if part % 8 == 0 else 1
    nx, ny = place.nx, place.ny
    dma = pltpu.SemaphoreType.DMA
    return pl.pallas_call(
        functools.partial(gather_kernel, place, pieces),
        in_specs=[pl.BlockSpec(memory_space=pltpu.VMEM)],
        out_specs=pl.BlockSpec(memory_space=pltpu.VMEM),
        out_shape=jax.ShapeDtypeStruct((tiles * nx * 2, side, side), mine.dtype),
        scratch_shapes=[
            dma((pieces,)),
            dma((nx - 1, pieces)),
            dma((nx - 1, pieces)),
            dma((nx - 1, ny - 1, pieces)),
            dma((nx - 1, ny - 1, pieces)),
            dma((nx - 1, ny, pieces)),
            dma((nx - 1, ny, pieces)),
            dma((pieces,)),
            dma((pieces,)),
        ],
        compiler_params=pltpu.CompilerParams(
            collective_id=1, has_side_effects=True, vmem_limit_bytes=24 * 2**20
        ),
        name="gather_tiles",
    )(mine)


def reduce_kernel(
    place,
    pieces,
    q,
    terms,
    out,
    own,
    mail,
    rc,
    sx,
    rx,
    sy,
    ry,
    sz,
    rz,
    done,
    own_sem,
    mail_sem,
    cs,
    cr,
    xs,
    xr,
    ys,
    yr,
    zs,
    zr,
    keep_sem,
    azs,
    azr,
    ays,
    ayr,
):
    me = place.locate()
    nx, ny, nz = me.nx, me.ny, me.nz
    other = me.at(c=1 - me.c)
    xp, yp, zp = me.x_peers(), me.y_peers(), me.z_peers()
    meet([other] + xp + yp + zp)
    started = []

    def go(copy):
        copy.start()
        started.append(copy)

    def wide(ref):
        return ref[...].astype(jnp.float32)

    def core_copy(p):
        return remote(mail.at[p], rc.at[p], cs.at[p], cr.at[p], other)

    def own_copy(p):
        return pltpu.make_async_copy(terms.at[me.c, p], own.at[p], own_sem.at[p])

    def mail_copy(p):
        return pltpu.make_async_copy(terms.at[1 - me.c, p], mail.at[p], mail_sem.at[p])

    def x_copy(p, k):
        return remote(sx.at[p, k - 1], rx.at[p, k - 1], xs.at[p, k - 1], xr.at[p, k - 1], xp[k - 1])

    def y_copy(p, j):
        return remote(sy.at[p, j - 1], ry.at[p, j - 1], ys.at[p, j - 1], yr.at[p, j - 1], yp[j - 1])

    def z_copy(p, m):
        return remote(sz.at[p, m - 1], rz.at[p, m - 1], zs.at[p, m - 1], zr.at[p, m - 1], zp[m - 1])

    def spread_z(p, m, z):
        return remote(
            done.at[p], out.at[p, me.y, z], azs.at[p, m - 1], azr.at[p, m - 1], zp[m - 1]
        )

    def spread_y(p, j, m, src, y, z):
        return remote(
            src, out.at[p, y, z], ays.at[p, j - 1, m], ayr.at[p, j - 1, m], yp[j - 1]
        )

    def keep_copy(p):
        return pltpu.make_async_copy(done.at[p], out.at[p, me.y, me.z], keep_sem.at[p])

    def over_x(p):
        own_copy(p).wait()
        core_copy(p).wait_recv()
        if p + WINDOW < pieces:
            core_copy(p).wait_send()
            mail_copy(p + WINDOW).wait()
            core_copy(p + WINDOW).start()
        for k in range(1, nx):
            x = me.step_x(k)

            def body(n, carry):
                total = wide(own.at[p, x, n]) + wide(rc.at[p, x, n])
                sx[p, k - 1, n] = total.astype(jnp.bfloat16)
                return carry

            lax.fori_loop(0, ny * nz * q, body, 0)
            go(x_copy(p, k))

    def up_to_x(p, n):
        total = wide(own.at[p, me.x, n]) + wide(rc.at[p, me.x, n])
        for k in range(1, nx):
            total = total + wide(rx.at[p, k - 1, n])
        return total

    def up_to_y(p, n):
        total = up_to_x(p, me.y * (nz * q) + n)
        for j in range(1, ny):
            total = total + wide(ry.at[p, j - 1, n])
        return total

    def over_y(p):
        for k in range(1, nx):
            x_copy(p, k).wait_recv()
        for j in range(1, ny):
            first = me.step_y(j) * (nz * q)

            def body(n, carry):
                sy[p, j - 1, n] = up_to_x(p, first + n).astype(jnp.bfloat16)
                return carry

            lax.fori_loop(0, nz * q, body, 0)
            go(y_copy(p, j))

    def over_z(p):
        for j in range(1, ny):
            y_copy(p, j).wait_recv()
        for m in range(1, nz):
            first = me.step_z(m) * q

            def body(i, carry):
                sz[p, m - 1, i] = up_to_y(p, first + i).astype(jnp.bfloat16)
                return carry

            lax.fori_loop(0, q, body, 0)
            go(z_copy(p, m))

    def finish(p):
        for m in range(1, nz):
            z_copy(p, m).wait_recv()

        def body(i, carry):
            total = up_to_y(p, me.z * q + i)
            for m in range(1, nz):
                total = total + wide(rz.at[p, m - 1, i])
            scale = lax.rsqrt(jnp.mean(total * total, keepdims=True) + 1e-06)
            done[p, i] = (total * scale).astype(jnp.bfloat16)
            return carry

        lax.fori_loop(0, q, body, 0)
        for m in range(1, nz):
            go(spread_z(p, m, me.z))
        for j in range(1, ny):
            go(spread_y(p, j, 0, done.at[p], me.y, me.z))
        keep_copy(p).start()

    def pass_on(p):
        for m in range(1, nz):
            z = me.step_z(-m)
            spread_z(p, m, z).wait_recv()
            for j in range(1, ny):
                go(spread_y(p, j, m, out.at[p, me.y, z], me.y, z))

    def collect(p):
        for j in range(1, ny):
            y = me.step_y(-j)
            for m in range(nz):
                z = me.step_z(-m)
                spread_y(p, j, m, done.at[p], y, z).wait_recv()

    for p in range(pieces):
        mail_copy(p).start()
        own_copy(p).start()
    for p in range(min(WINDOW, pieces)):
        mail_copy(p).wait()
        core_copy(p).start()
    stages = [over_x, over_y, over_z, finish, pass_on, collect]
    for t in range(pieces + len(stages) - 1):
        for s, stage in enumerate(stages):
            if 0 <= t - s < pieces:
                stage(t - s)
    for p in range(pieces):
        keep_copy(p).wait()
        if p + WINDOW >= pieces:
            core_copy(p).wait_send()
    for copy in started:
        copy.wait_send()


def reduce_terms(terms, place, pieces, q):
    side = terms.shape[-1]
    nx, ny, nz = place.nx, place.ny, place.nz
    n = ny * nz * q
    dma = pltpu.SemaphoreType.DMA

    def room(*lead, dtype=jnp.bfloat16):
        return pltpu.VMEM((pieces,) + lead + (side, side), dtype)

    return pl.pallas_call(
        functools.partial(reduce_kernel, place, pieces, q),
        in_specs=[pl.BlockSpec(memory_space=pl.ANY)],
        out_specs=pl.BlockSpec(memory_space=pltpu.VMEM),
        out_shape=jax.ShapeDtypeStruct((pieces, ny, nz, q, side, side), jnp.bfloat16),
        scratch_shapes=[
            room(nx, n, dtype=jnp.float32),
            room(nx, n, dtype=jnp.float32),
            room(nx, n, dtype=jnp.float32),
            room(nx - 1, n),
            room(nx - 1, n),
            room(ny - 1, nz * q),
            room(ny - 1, nz * q),
            room(nz - 1, q),
            room(nz - 1, q),
            room(q),
            dma((pieces,)),
            dma((pieces,)),
            dma((pieces,)),
            dma((pieces,)),
            dma((pieces, nx - 1)),
            dma((pieces, nx - 1)),
            dma((pieces, ny - 1)),
            dma((pieces, ny - 1)),
            dma((pieces, nz - 1)),
            dma((pieces, nz - 1)),
            dma((pieces,)),
            dma((pieces, nz - 1)),
            dma((pieces, nz - 1)),
            dma((pieces, ny - 1, nz)),
            dma((pieces, ny - 1, nz)),
        ],
        compiler_params=pltpu.CompilerParams(
            collective_id=2, has_side_effects=True, vmem_limit_bytes=48 * 2**20
        ),
        name="reduce_terms",
    )(terms)


def on_device(n_dp, n_fsdp, features, grad_out, weight_tiles, tile_row, tile_column):
    tiles_here, side, _ = weight_tiles.shape
    nblocks = features.shape[1] // side
    place = Place(n_dp, n_fsdp)
    nx, n = place.nx, place.ny * place.nz
    pieces = max(count for count in (1, 2, 4, 8) if tiles_here % (n * count) == 0)
    n = tiles_here // pieces
    blocks, tiles = pattern(tile_row, tile_column, nblocks)
    owner, rest = tiles // tiles_here, tiles % tiles_here
    places = ((owner % 2 * pieces + rest // n) * nx + owner // 2) * n + rest % n
    whole = gather_tiles(weight_tiles, place)
    grad_features, partial = layer(features, grad_out, whole, blocks, tiles, places)
    terms = partial.reshape(2, pieces, nx, n, side, side)
    tile_update = reduce_terms(terms, place, pieces, n // (place.ny * place.nz))
    return (grad_features, tile_update.reshape(tiles_here, side, side).astype(jnp.float32))


def solution(mesh):
    return jax.shard_map(
        functools.partial(on_device, mesh.shape["dp"], mesh.shape["fsdp"]),
        mesh=mesh,
        in_specs=(
            P(("dp", "fsdp"), None),
            P(("dp", "fsdp"), None),
            P("fsdp", None, None),
            P(),
            P(),
        ),
        out_specs=(P(("dp", "fsdp"), None), P("fsdp", None, None)),
        check_vma=False,
    )
```

```python
import functools
import math

import jax
import jax.numpy as jnp
from jax import lax
from jax.experimental import pallas as pl
from jax.experimental.pallas import tpu as pltpu
from jax.sharding import PartitionSpec as P

SIDE_BLOCKS = 4
MESH = pl.DeviceIdType.MESH
WINDOW = 3
ROOT = math.sqrt(2.0 / math.pi)


def gelu_slope(value):
    square = value * value
    half = 0.5 + 0.5 * jnp.tanh(value * (ROOT + (0.044715 * ROOT) * square))
    return half + half * (1.0 - half) * (value * (2.0 * ROOT + (6.0 * 0.044715 * ROOT) * square))


def pattern(tile_row, tile_column, nblocks):
    total = tile_row.shape[0]
    mask = jnp.max(jnp.bitwise_xor(tile_row, tile_column))
    ids = jnp.arange(nblocks, dtype=jnp.int32)
    keys = jnp.bitwise_and(ids, ~mask) * nblocks + jnp.bitwise_and(ids, mask)

    def place(block):
        key = jnp.bitwise_and(block, ~mask) * nblocks + jnp.bitwise_and(block, mask)
        return jnp.sum((keys[None, :] < key[:, None]).astype(jnp.int32), axis=1)

    places = place(ids)
    blocks = jnp.sum(jnp.where(places[None, :] == ids[:, None], ids[None, :], 0), axis=1)
    at_row, at_column = place(tile_row), place(tile_column)
    slots = at_column * SIDE_BLOCKS + at_row % SIDE_BLOCKS
    every = jnp.arange(total, dtype=jnp.int32)
    tiles = jnp.sum(jnp.where(slots[None, :] == every[:, None], every[None, :], 0), axis=1)
    return blocks, tiles


def layer_kernel(steps, blocks, tiles, places, features, grads, whole, out_ref, partial_ref, term_buf, sems):
    n, m = SIDE_BLOCKS, SIDE_BLOCKS * SIDE_BLOCKS
    side = whole.shape[1]

    def drain(slot):
        pltpu.make_async_copy(
            term_buf.at[slot], partial_ref.at[pl.ds(0, m)], sems.at[slot]
        ).wait()

    def group(g, slot):
        columns = [
            pl.ds(pl.multiple_of(blocks[g * n + k] * side, side), side) for k in range(n)
        ]
        feature = jnp.concatenate([features[:, at] for at in columns], axis=1)
        grad = jnp.concatenate([grads[:, at] for at in columns], axis=1).astype(jnp.float32)
        weight = jnp.concatenate(
            [
                jnp.concatenate([whole[tiles[g * m + c * n + r]] for r in range(n)], axis=1)
                for c in range(n)
            ],
            axis=0,
        )
        preact = jnp.dot(feature, weight, preferred_element_type=jnp.float32)
        slope = (grad * gelu_slope(preact)).astype(jnp.bfloat16)
        back = lax.dot_general(
            slope, weight, (((1,), (1,)), ((), ())), preferred_element_type=jnp.float32
        )
        term = lax.dot_general(
            feature, slope, (((0,), (0,)), ((), ())), preferred_element_type=jnp.float32
        )
        return columns, (grad + back).astype(jnp.bfloat16), term

    slots = term_buf.shape[0]

    def body(i, carry):
        @pl.when(i > 0)
        def _():
            for slot in range(slots):
                drain(slot)

        found = [group(i * slots + slot, slot) for slot in range(slots)]
        for slot, (columns, result, term) in enumerate(found):
            for k, at in enumerate(columns):
                out_ref[:, at] = result[:, k * side : (k + 1) * side]
            for c in range(n):
                for r in range(n):
                    term_buf[slot, c * n + r] = term[
                        c * side : (c + 1) * side, r * side : (r + 1) * side
                    ]
        for slot in range(slots):
            for k in range(m):
                pltpu.make_async_copy(
                    term_buf.at[slot, k],
                    partial_ref.at[places[(i * slots + slot) * m + k]],
                    sems.at[slot],
                ).start()
        return carry

    lax.fori_loop(0, steps // slots, body, 0)
    for slot in range(slots):
        drain(slot)


def layer(features, grad_out, whole, blocks, tiles, places):
    rows, width = features.shape
    total, side, _ = whole.shape
    n, m = SIDE_BLOCKS, SIDE_BLOCKS * SIDE_BLOCKS
    steps = width // side // n
    slots = 2 if steps % 2 == 0 else 1
    vmem = pl.BlockSpec(memory_space=pltpu.VMEM)
    smem = pl.BlockSpec(memory_space=pltpu.SMEM)
    return pl.pallas_call(
        functools.partial(layer_kernel, steps),
        in_specs=[smem] * 3 + [vmem] * 3,
        out_specs=[vmem, pl.BlockSpec(memory_space=pl.ANY)],
        scratch_shapes=[
            pltpu.VMEM((slots, m, side, side), jnp.float32),
            pltpu.SemaphoreType.DMA((slots,)),
        ],
        out_shape=[
            jax.ShapeDtypeStruct((rows, width), jnp.bfloat16),
            jax.ShapeDtypeStruct((total, side, side), jnp.float32),
        ],
        compiler_params=pltpu.CompilerParams(vmem_limit_bytes=26 * 2**20),
        cost_estimate=pl.CostEstimate(
            flops=6 * rows * width * n * side,
            bytes_accessed=6 * rows * width + 6 * total * side * side,
            transcendentals=rows * width,
        ),
        name="layer",
    )(blocks, tiles, places, features, grad_out, whole)


class Place:
    def __init__(self, n_dp, n_fsdp):
        self.cores = 2
        self.nx = n_fsdp // 2
        self.ny = 2 if n_dp <= 8 else 4
        self.nz = n_dp // self.ny

    def locate(self):
        fsdp, dp = lax.axis_index("fsdp"), lax.axis_index("dp")
        self.x, self.c = fsdp // 2, fsdp % 2
        self.z, self.y = dp // self.ny, dp % self.ny
        return self

    def at(self, x=None, c=None, y=None, z=None):
        x = self.x if x is None else x
        c = self.c if c is None else c
        y = self.y if y is None else y
        z = self.z if z is None else z
        return (z * self.ny + y, x * 2 + c)

    def step_x(self, k):
        return lax.rem(self.x + k + self.nx, self.nx)

    def step_y(self, k):
        return lax.rem(self.y + k + self.ny, self.ny)

    def step_z(self, k):
        return lax.rem(self.z + k + self.nz, self.nz)

    def x_peers(self):
        return [self.at(x=self.step_x(k)) for k in range(1, self.nx)]

    def y_peers(self):
        return [self.at(y=self.step_y(k)) for k in range(1, self.ny)]

    def z_peers(self):
        return [self.at(z=self.step_z(k)) for k in range(1, self.nz)]


def meet(peers):
    barrier = pltpu.get_barrier_semaphore()
    for peer in peers:
        pl.semaphore_signal(barrier, inc=1, device_id=peer, device_id_type=MESH)
    pl.semaphore_wait(barrier, len(peers))


def remote(src, dst, send, recv, peer):
    return pltpu.make_async_remote_copy(
        src_ref=src, dst_ref=dst, send_sem=send, recv_sem=recv, device_id=peer, device_id_type=MESH
    )


def gather_kernel(
    place, nw, pieces, mine, whole, own_sem, xs, xr, ys, yr, zs, zr, ds, dr, cs, cr, ws, wr
):
    me = place.locate()
    nx, ny = me.nx, me.ny
    tiles = mine.shape[0]
    part = tiles // (ny * nw)
    q = part // pieces
    w = me.z % nw
    other = me.at(c=1 - me.c)
    xp, yp = me.x_peers(), me.y_peers()
    zp = me.at(z=me.z + 1 - 2 * w) if nw == 2 else None
    meet(xp + yp + [other] + ([zp] if nw == 2 else []))
    run = ny * nw * q
    started = []

    def go(copy):
        copy.start()
        started.append(copy)

    def inner(y, v, p):
        return y * (nw * part) + v * part + p * q

    def span(x, y, v, p, core=None):
        core = me.c if core is None else core
        return whole.at[pl.ds((x * 2 + core) * tiles + inner(y, v, p), q)]

    def x_copy(p, k, x):
        return remote(
            mine.at[pl.ds(inner(me.y, w, p), q)],
            span(x, me.y, w, p),
            xs.at[k - 1, p],
            xr.at[k - 1, p],
            xp[k - 1],
        )

    def home(core, p):
        return whole.at[pl.ds((me.x * 2 + core) * tiles + p * run, run)]

    def own_copy(p):
        return pltpu.make_async_copy(mine.at[pl.ds(p * run, run)], home(me.c, p), own_sem.at[p])

    def core_copy(p, core):
        return remote(mine.at[pl.ds(p * run, run)], home(core, p), ws.at[p], wr.at[p], other)

    def in_chip(k, j, v, p, at):
        return remote(at, at, cs.at[k - 1, j, v, p], cr.at[k - 1, j, v, p], other)

    def y_copy(k, j, y, p):
        at = span(me.step_x(-k), y, w, p)
        return remote(at, at, ys.at[k - 1, j - 1, p], yr.at[k - 1, j - 1, p], yp[j - 1])

    def z_copy(k, v, p):
        at = span(me.step_x(-k), me.y, v, p)
        return remote(at, at, zs.at[k - 1, p], zr.at[k - 1, p], zp)

    def last_copy(k, j, y, v, p):
        at = span(me.step_x(-k), y, v, p)
        peer = zp if p % 2 == 0 else yp[j - 1]
        return remote(at, at, ds.at[k - 1, j - 1, p], dr.at[k - 1, j - 1, p], peer)

    def land_x(p):
        for k in range(1, nx):
            x = me.step_x(-k)
            x_copy(p, k, x).wait_recv()
            for j in range(1, ny):
                go(y_copy(k, j, me.y, p))
            if nw == 2:
                go(z_copy(k, w, p))
            go(in_chip(k, 0, 0, p, span(x, me.y, w, p)))
            x_copy(p, k, me.x).wait_send()
            if p + WINDOW < pieces:
                x_copy(p + WINDOW, k, me.x).start()
        go(core_copy(p, me.c))
        own_copy(p).start()

    def land_yz(p):
        for k in range(1, nx):
            x = me.step_x(-k)
            for j in range(1, ny):
                y = me.step_y(-j)
                y_copy(k, j, y, p).wait_recv()
                if nw == 2 and p % 2 == 0:
                    go(last_copy(k, j, y, w, p))
                go(in_chip(k, j, 0, p, span(x, y, w, p)))
            if nw == 2:
                z_copy(k, 1 - w, p).wait_recv()
                if p % 2 == 1:
                    for j in range(1, ny):
                        go(last_copy(k, j, me.y, 1 - w, p))
                go(in_chip(k, 0, 1, p, span(x, me.y, 1 - w, p)))

    def land_last(p):
        for k in range(1, nx):
            x = me.step_x(-k)
            for j in range(1, ny):
                y = me.step_y(-j)
                last_copy(k, j, y, 1 - w, p).wait_recv()
                go(in_chip(k, j, 1, p, span(x, y, 1 - w, p)))

    for p in range(min(WINDOW, pieces)):
        for k in range(1, nx):
            x_copy(p, k, me.x).start()
    stages = [land_x, land_yz] + ([land_last] if nw == 2 else [])
    for t in range(pieces + len(stages) - 1):
        for s, stage in enumerate(stages):
            if 0 <= t - s < pieces:
                stage(t - s)
    for p in range(pieces):
        own_copy(p).wait()
        core_copy(p, 1 - me.c).wait_recv()
        for k in range(1, nx):
            x = me.step_x(-k)
            for j in range(ny):
                y = me.step_y(-j)
                for v in range(nw):
                    u = w if v == 0 else 1 - w
                    in_chip(k, j, v, p, span(x, y, u, p, 1 - me.c)).wait_recv()
    for copy in started:
        copy.wait_send()


def gather_tiles(mine, place):
    tiles, side, _ = mine.shape
    nx, ny = place.nx, place.ny
    nw = 2 if place.nz % 2 == 0 and tiles % (2 * ny) == 0 else 1
    part = tiles // (ny * nw)
    pieces = 4 if part % 4 == 0 else 1
    dma = pltpu.SemaphoreType.DMA
    return pl.pallas_call(
        functools.partial(gather_kernel, place, nw, pieces),
        in_specs=[pl.BlockSpec(memory_space=pltpu.VMEM)],
        out_specs=pl.BlockSpec(memory_space=pltpu.VMEM),
        out_shape=jax.ShapeDtypeStruct((tiles * nx * 2, side, side), mine.dtype),
        scratch_shapes=[dma((pieces,))]
        + [dma((nx - 1, pieces))] * 2
        + [dma((nx - 1, ny - 1, pieces))] * 2
        + [dma((nx - 1, pieces))] * 2
        + [dma((nx - 1, ny - 1, pieces))] * 2
        + [dma((nx - 1, ny, nw, pieces))] * 2
        + [dma((pieces,))] * 2,
        compiler_params=pltpu.CompilerParams(
            collective_id=1, has_side_effects=True, vmem_limit_bytes=24 * 2**20
        ),
        name="gather_tiles",
    )(mine)


def reduce_kernel(
    place,
    pieces,
    q,
    terms,
    out,
    own,
    rc,
    sx,
    rx,
    sy,
    ry,
    sz,
    rz,
    done,
    own_sem,
    cs,
    cr,
    xs,
    xr,
    ys,
    yr,
    zs,
    zr,
    keep_sem,
    azs,
    azr,
    ays,
    ayr,
):
    me = place.locate()
    nx, ny, nz = me.nx, me.ny, me.nz
    other = me.at(c=1 - me.c)
    xp, yp, zp = me.x_peers(), me.y_peers(), me.z_peers()
    meet([other] + xp + yp + zp)
    started = []

    def go(copy):
        copy.start()
        started.append(copy)

    def wide(ref):
        return ref[...].astype(jnp.float32)

    def core_copy(p):
        return remote(terms.at[1 - me.c, p], rc.at[p], cs.at[p], cr.at[p], other)

    def own_copy(p):
        return pltpu.make_async_copy(terms.at[me.c, p], own.at[p], own_sem.at[p])

    def x_copy(p, k):
        return remote(sx.at[p, k - 1], rx.at[p, k - 1], xs.at[p, k - 1], xr.at[p, k - 1], xp[k - 1])

    def y_copy(p, j):
        return remote(sy.at[p, j - 1], ry.at[p, j - 1], ys.at[p, j - 1], yr.at[p, j - 1], yp[j - 1])

    def z_copy(p, m):
        return remote(sz.at[p, m - 1], rz.at[p, m - 1], zs.at[p, m - 1], zr.at[p, m - 1], zp[m - 1])

    def spread_z(p, m, z):
        return remote(
            done.at[p], out.at[p, me.y, z], azs.at[p, m - 1], azr.at[p, m - 1], zp[m - 1]
        )

    def spread_y(p, j, m, src, y, z):
        return remote(
            src, out.at[p, y, z], ays.at[p, j - 1, m], ayr.at[p, j - 1, m], yp[j - 1]
        )

    def keep_copy(p):
        return pltpu.make_async_copy(done.at[p], out.at[p, me.y, me.z], keep_sem.at[p])

    def over_x(p):
        own_copy(p).wait()
        core_copy(p).wait_recv()
        if p + WINDOW < pieces:
            core_copy(p).wait_send()
            core_copy(p + WINDOW).start()
            own_copy(p + WINDOW).start()
        for k in range(1, nx):
            x = me.step_x(k)

            def body(n, carry):
                total = wide(own.at[p, x, n]) + wide(rc.at[p, x, n])
                sx[p, k - 1, n] = total.astype(jnp.bfloat16)
                return carry

            lax.fori_loop(0, ny * nz * q, body, 0)
            go(x_copy(p, k))

    def up_to_x(p, n):
        total = wide(own.at[p, me.x, n]) + wide(rc.at[p, me.x, n])
        for k in range(1, nx):
            total = total + wide(rx.at[p, k - 1, n])
        return total

    def up_to_y(p, n):
        total = up_to_x(p, me.y * (nz * q) + n)
        for j in range(1, ny):
            total = total + wide(ry.at[p, j - 1, n])
        return total

    def over_y(p):
        for k in range(1, nx):
            x_copy(p, k).wait_recv()
        for j in range(1, ny):
            first = me.step_y(j) * (nz * q)

            def body(n, carry):
                sy[p, j - 1, n] = up_to_x(p, first + n).astype(jnp.bfloat16)
                return carry

            lax.fori_loop(0, nz * q, body, 0)
            go(y_copy(p, j))

    def over_z(p):
        for j in range(1, ny):
            y_copy(p, j).wait_recv()
        for m in range(1, nz):
            first = me.step_z(m) * q

            def body(i, carry):
                sz[p, m - 1, i] = up_to_y(p, first + i).astype(jnp.bfloat16)
                return carry

            lax.fori_loop(0, q, body, 0)
            go(z_copy(p, m))

    def finish(p):
        for m in range(1, nz):
            z_copy(p, m).wait_recv()

        def body(i, carry):
            total = up_to_y(p, me.z * q + i)
            for m in range(1, nz):
                total = total + wide(rz.at[p, m - 1, i])
            scale = lax.rsqrt(jnp.mean(total * total, keepdims=True) + 1e-06)
            done[p, i] = (total * scale).astype(jnp.bfloat16)
            return carry

        lax.fori_loop(0, q, body, 0)
        for m in range(1, nz):
            go(spread_z(p, m, me.z))
        for j in range(1, ny):
            go(spread_y(p, j, 0, done.at[p], me.y, me.z))
        keep_copy(p).start()

    def pass_on(p):
        for m in range(1, nz):
            z = me.step_z(-m)
            spread_z(p, m, z).wait_recv()
            for j in range(1, ny):
                go(spread_y(p, j, m, out.at[p, me.y, z], me.y, z))

    def collect(p):
        for j in range(1, ny):
            y = me.step_y(-j)
            for m in range(nz):
                z = me.step_z(-m)
                spread_y(p, j, m, done.at[p], y, z).wait_recv()

    for p in range(min(WINDOW, pieces)):
        core_copy(p).start()
        own_copy(p).start()
    stages = [over_x, over_y, over_z, finish, pass_on, collect]
    for t in range(pieces + len(stages) - 1):
        for s, stage in enumerate(stages):
            if 0 <= t - s < pieces:
                stage(t - s)
    for p in range(pieces):
        keep_copy(p).wait()
        if p + WINDOW >= pieces:
            core_copy(p).wait_send()
    for copy in started:
        copy.wait_send()


def reduce_terms(terms, place, pieces, q):
    side = terms.shape[-1]
    nx, ny, nz = place.nx, place.ny, place.nz
    n = ny * nz * q
    dma = pltpu.SemaphoreType.DMA

    def room(*lead, dtype=jnp.bfloat16):
        return pltpu.VMEM((pieces,) + lead + (side, side), dtype)

    return pl.pallas_call(
        functools.partial(reduce_kernel, place, pieces, q),
        in_specs=[pl.BlockSpec(memory_space=pl.ANY)],
        out_specs=pl.BlockSpec(memory_space=pl.ANY),
        out_shape=jax.ShapeDtypeStruct((pieces, ny, nz, q, side, side), jnp.bfloat16),
        scratch_shapes=[
            room(nx, n, dtype=jnp.float32),
            room(nx, n, dtype=jnp.float32),
            room(nx - 1, n),
            room(nx - 1, n),
            room(ny - 1, nz * q),
            room(ny - 1, nz * q),
            room(nz - 1, q),
            room(nz - 1, q),
            room(q),
            dma((pieces,)),
            dma((pieces,)),
            dma((pieces,)),
            dma((pieces, nx - 1)),
            dma((pieces, nx - 1)),
            dma((pieces, ny - 1)),
            dma((pieces, ny - 1)),
            dma((pieces, nz - 1)),
            dma((pieces, nz - 1)),
            dma((pieces,)),
            dma((pieces, nz - 1)),
            dma((pieces, nz - 1)),
            dma((pieces, ny - 1, nz)),
            dma((pieces, ny - 1, nz)),
        ],
        compiler_params=pltpu.CompilerParams(
            collective_id=2, has_side_effects=True, vmem_limit_bytes=48 * 2**20
        ),
        name="reduce_terms",
    )(terms)


def on_device(n_dp, n_fsdp, features, grad_out, weight_tiles, tile_row, tile_column):
    tiles_here, side, _ = weight_tiles.shape
    nblocks = features.shape[1] // side
    place = Place(n_dp, n_fsdp)
    nx, n = place.nx, place.ny * place.nz
    pieces = max(count for count in (1, 2, 4, 8) if tiles_here % (n * count) == 0)
    n = tiles_here // pieces
    blocks, tiles = pattern(tile_row, tile_column, nblocks)
    owner, rest = tiles // tiles_here, tiles % tiles_here
    places = ((owner % 2 * pieces + rest // n) * nx + owner // 2) * n + rest % n
    whole = gather_tiles(weight_tiles, place)
    grad_features, partial = layer(features, grad_out, whole, blocks, tiles, places)
    terms = partial.reshape(2, pieces, nx, n, side, side)
    tile_update = reduce_terms(terms, place, pieces, n // (place.ny * place.nz))
    return (grad_features, tile_update.reshape(tiles_here, side, side).astype(jnp.float32))


def solution(mesh):
    return jax.shard_map(
        functools.partial(on_device, mesh.shape["dp"], mesh.shape["fsdp"]),
        mesh=mesh,
        in_specs=(
            P(("dp", "fsdp"), None),
            P(("dp", "fsdp"), None),
            P("fsdp", None, None),
            P(),
            P(),
        ),
        out_specs=(P(("dp", "fsdp"), None), P("fsdp", None, None)),
        check_vma=False,
    )
```

```python
import functools
import math

import jax
import jax.numpy as jnp
from jax import lax
from jax.experimental import pallas as pl
from jax.experimental.pallas import tpu as pltpu
from jax.sharding import PartitionSpec as P

SIDE_BLOCKS = 4
MESH = pl.DeviceIdType.MESH
WINDOW = 3
ROOT = math.sqrt(2.0 / math.pi)


def gelu_slope(value):
    square = value * value
    half = 0.5 + 0.5 * jnp.tanh(value * (ROOT + (0.044715 * ROOT) * square))
    return half + half * (1.0 - half) * (value * (2.0 * ROOT + (6.0 * 0.044715 * ROOT) * square))


def pattern(tile_row, tile_column, nblocks):
    total = tile_row.shape[0]
    mask = jnp.max(jnp.bitwise_xor(tile_row, tile_column))
    ids = jnp.arange(nblocks, dtype=jnp.int32)
    keys = jnp.bitwise_and(ids, ~mask) * nblocks + jnp.bitwise_and(ids, mask)

    def place(block):
        key = jnp.bitwise_and(block, ~mask) * nblocks + jnp.bitwise_and(block, mask)
        return jnp.sum((keys[None, :] < key[:, None]).astype(jnp.int32), axis=1)

    places = place(ids)
    blocks = jnp.sum(jnp.where(places[None, :] == ids[:, None], ids[None, :], 0), axis=1)
    at_row, at_column = place(tile_row), place(tile_column)
    slots = at_column * SIDE_BLOCKS + at_row % SIDE_BLOCKS
    every = jnp.arange(total, dtype=jnp.int32)
    tiles = jnp.sum(jnp.where(slots[None, :] == every[:, None], every[None, :], 0), axis=1)
    return blocks, tiles


def layer_kernel(steps, blocks, tiles, places, features, grads, whole, out_ref, partial_ref, term_buf, sems):
    n, m = SIDE_BLOCKS, SIDE_BLOCKS * SIDE_BLOCKS
    side = whole.shape[1]

    def drain(slot):
        pltpu.make_async_copy(
            term_buf.at[slot], partial_ref.at[pl.ds(0, m)], sems.at[slot]
        ).wait()

    def group(g, slot):
        columns = [
            pl.ds(pl.multiple_of(blocks[g * n + k] * side, side), side) for k in range(n)
        ]
        feature = jnp.concatenate([features[:, at] for at in columns], axis=1)
        grad = jnp.concatenate([grads[:, at] for at in columns], axis=1).astype(jnp.float32)
        weight = jnp.concatenate(
            [
                jnp.concatenate([whole[tiles[g * m + c * n + r]] for r in range(n)], axis=1)
                for c in range(n)
            ],
            axis=0,
        )
        preact = jnp.dot(feature, weight, preferred_element_type=jnp.float32)
        slope = (grad * gelu_slope(preact)).astype(jnp.bfloat16)
        back = lax.dot_general(
            slope, weight, (((1,), (1,)), ((), ())), preferred_element_type=jnp.float32
        )
        result = (grad + back).astype(jnp.bfloat16)
        for k, at in enumerate(columns):
            out_ref[:, at] = result[:, k * side : (k + 1) * side]
        term = lax.dot_general(
            feature, slope, (((0,), (0,)), ((), ())), preferred_element_type=jnp.float32
        )
        for c in range(n):
            for r in range(n):
                term_buf[slot, c * n + r] = term[
                    c * side : (c + 1) * side, r * side : (r + 1) * side
                ]
        for k in range(m):
            pltpu.make_async_copy(
                term_buf.at[slot, k], partial_ref.at[places[g * m + k]], sems.at[slot]
            ).start()

    slots = term_buf.shape[0]

    def body(i, carry):
        for k in range(slots):

            @pl.when(i > 0)
            def _():
                drain(k)

            group(i * slots + k, k)
        return carry

    lax.fori_loop(0, steps // slots, body, 0)
    for k in range(slots):
        drain(k)


def layer(features, grad_out, whole, blocks, tiles, places):
    rows, width = features.shape
    total, side, _ = whole.shape
    n, m = SIDE_BLOCKS, SIDE_BLOCKS * SIDE_BLOCKS
    steps = width // side // n
    slots = 2 if steps % 2 == 0 else 1
    vmem = pl.BlockSpec(memory_space=pltpu.VMEM)
    smem = pl.BlockSpec(memory_space=pltpu.SMEM)
    return pl.pallas_call(
        functools.partial(layer_kernel, steps),
        in_specs=[smem] * 3 + [vmem] * 3,
        out_specs=[vmem, pl.BlockSpec(memory_space=pl.ANY)],
        scratch_shapes=[
            pltpu.VMEM((slots, m, side, side), jnp.float32),
            pltpu.SemaphoreType.DMA((slots,)),
        ],
        out_shape=[
            jax.ShapeDtypeStruct((rows, width), jnp.bfloat16),
            jax.ShapeDtypeStruct((total, side, side), jnp.float32),
        ],
        compiler_params=pltpu.CompilerParams(vmem_limit_bytes=26 * 2**20),
        cost_estimate=pl.CostEstimate(
            flops=6 * rows * width * n * side,
            bytes_accessed=6 * rows * width + 6 * total * side * side,
            transcendentals=rows * width,
        ),
        name="layer",
    )(blocks, tiles, places, features, grad_out, whole)


class Place:
    def __init__(self, n_dp, n_fsdp):
        self.cores = 2
        self.nx = n_fsdp // 2
        self.ny = 2 if n_dp <= 8 else 4
        self.nz = n_dp // self.ny

    def locate(self):
        fsdp, dp = lax.axis_index("fsdp"), lax.axis_index("dp")
        self.x, self.c = fsdp // 2, fsdp % 2
        self.z, self.y = dp // self.ny, dp % self.ny
        return self

    def at(self, x=None, c=None, y=None, z=None):
        x = self.x if x is None else x
        c = self.c if c is None else c
        y = self.y if y is None else y
        z = self.z if z is None else z
        return (z * self.ny + y, x * 2 + c)

    def step_x(self, k):
        return lax.rem(self.x + k + self.nx, self.nx)

    def step_y(self, k):
        return lax.rem(self.y + k + self.ny, self.ny)

    def step_z(self, k):
        return lax.rem(self.z + k + self.nz, self.nz)

    def x_peers(self):
        return [self.at(x=self.step_x(k)) for k in range(1, self.nx)]

    def y_peers(self):
        return [self.at(y=self.step_y(k)) for k in range(1, self.ny)]

    def z_peers(self):
        return [self.at(z=self.step_z(k)) for k in range(1, self.nz)]


def meet(peers):
    barrier = pltpu.get_barrier_semaphore()
    for peer in peers:
        pl.semaphore_signal(barrier, inc=1, device_id=peer, device_id_type=MESH)
    pl.semaphore_wait(barrier, len(peers))


def remote(src, dst, send, recv, peer):
    return pltpu.make_async_remote_copy(
        src_ref=src, dst_ref=dst, send_sem=send, recv_sem=recv, device_id=peer, device_id_type=MESH
    )


def gather_kernel(
    place, nw, pieces, mine, whole, own_sem, xs, xr, ys, yr, zs, zr, ds, dr, cs, cr, ws, wr
):
    me = place.locate()
    nx, ny = me.nx, me.ny
    tiles = mine.shape[0]
    part = tiles // (ny * nw)
    q = part // pieces
    w = me.z % nw
    other = me.at(c=1 - me.c)
    xp, yp = me.x_peers(), me.y_peers()
    zp = me.at(z=me.z + 1 - 2 * w) if nw == 2 else None
    meet(xp + yp + [other] + ([zp] if nw == 2 else []))
    run = ny * nw * q
    started = []

    def go(copy):
        copy.start()
        started.append(copy)

    def inner(y, v, p):
        return y * (nw * part) + v * part + p * q

    def span(x, y, v, p, core=None):
        core = me.c if core is None else core
        return whole.at[pl.ds((x * 2 + core) * tiles + inner(y, v, p), q)]

    def x_copy(p, k, x):
        return remote(
            mine.at[pl.ds(inner(me.y, w, p), q)],
            span(x, me.y, w, p),
            xs.at[k - 1, p],
            xr.at[k - 1, p],
            xp[k - 1],
        )

    def home(core, p):
        return whole.at[pl.ds((me.x * 2 + core) * tiles + p * run, run)]

    def own_copy(p):
        return pltpu.make_async_copy(mine.at[pl.ds(p * run, run)], home(me.c, p), own_sem.at[p])

    def core_copy(p, core):
        return remote(mine.at[pl.ds(p * run, run)], home(core, p), ws.at[p], wr.at[p], other)

    def in_chip(k, j, v, p, at):
        return remote(at, at, cs.at[k - 1, j, v, p], cr.at[k - 1, j, v, p], other)

    def y_copy(k, j, y, p):
        at = span(me.step_x(-k), y, w, p)
        return remote(at, at, ys.at[k - 1, j - 1, p], yr.at[k - 1, j - 1, p], yp[j - 1])

    def z_copy(k, v, p):
        at = span(me.step_x(-k), me.y, v, p)
        return remote(at, at, zs.at[k - 1, p], zr.at[k - 1, p], zp)

    def last_copy(k, j, y, v, p):
        at = span(me.step_x(-k), y, v, p)
        peer = zp if p % 2 == 0 else yp[j - 1]
        return remote(at, at, ds.at[k - 1, j - 1, p], dr.at[k - 1, j - 1, p], peer)

    def land_x(p):
        for k in range(1, nx):
            x = me.step_x(-k)
            x_copy(p, k, x).wait_recv()
            for j in range(1, ny):
                go(y_copy(k, j, me.y, p))
            if nw == 2:
                go(z_copy(k, w, p))
            go(in_chip(k, 0, 0, p, span(x, me.y, w, p)))
            x_copy(p, k, me.x).wait_send()
            if p + WINDOW < pieces:
                x_copy(p + WINDOW, k, me.x).start()
        go(core_copy(p, me.c))
        own_copy(p).start()

    def land_yz(p):
        for k in range(1, nx):
            x = me.step_x(-k)
            for j in range(1, ny):
                y = me.step_y(-j)
                y_copy(k, j, y, p).wait_recv()
                if nw == 2 and p % 2 == 0:
                    go(last_copy(k, j, y, w, p))
                go(in_chip(k, j, 0, p, span(x, y, w, p)))
            if nw == 2:
                z_copy(k, 1 - w, p).wait_recv()
                if p % 2 == 1:
                    for j in range(1, ny):
                        go(last_copy(k, j, me.y, 1 - w, p))
                go(in_chip(k, 0, 1, p, span(x, me.y, 1 - w, p)))

    def land_last(p):
        for k in range(1, nx):
            x = me.step_x(-k)
            for j in range(1, ny):
                y = me.step_y(-j)
                last_copy(k, j, y, 1 - w, p).wait_recv()
                go(in_chip(k, j, 1, p, span(x, y, 1 - w, p)))

    for p in range(min(WINDOW, pieces)):
        for k in range(1, nx):
            x_copy(p, k, me.x).start()
    stages = [land_x, land_yz] + ([land_last] if nw == 2 else [])
    for t in range(pieces + len(stages) - 1):
        for s, stage in enumerate(stages):
            if 0 <= t - s < pieces:
                stage(t - s)
    for p in range(pieces):
        own_copy(p).wait()
        core_copy(p, 1 - me.c).wait_recv()
        for k in range(1, nx):
            x = me.step_x(-k)
            for j in range(ny):
                y = me.step_y(-j)
                for v in range(nw):
                    u = w if v == 0 else 1 - w
                    in_chip(k, j, v, p, span(x, y, u, p, 1 - me.c)).wait_recv()
    for copy in started:
        copy.wait_send()


def gather_tiles(mine, place):
    tiles, side, _ = mine.shape
    nx, ny = place.nx, place.ny
    nw = 2 if place.nz % 2 == 0 and tiles % (2 * ny) == 0 else 1
    part = tiles // (ny * nw)
    pieces = 4 if part % 4 == 0 else 1
    dma = pltpu.SemaphoreType.DMA
    return pl.pallas_call(
        functools.partial(gather_kernel, place, nw, pieces),
        in_specs=[pl.BlockSpec(memory_space=pltpu.VMEM)],
        out_specs=pl.BlockSpec(memory_space=pltpu.VMEM),
        out_shape=jax.ShapeDtypeStruct((tiles * nx * 2, side, side), mine.dtype),
        scratch_shapes=[dma((pieces,))]
        + [dma((nx - 1, pieces))] * 2
        + [dma((nx - 1, ny - 1, pieces))] * 2
        + [dma((nx - 1, pieces))] * 2
        + [dma((nx - 1, ny - 1, pieces))] * 2
        + [dma((nx - 1, ny, nw, pieces))] * 2
        + [dma((pieces,))] * 2,
        compiler_params=pltpu.CompilerParams(
            collective_id=1, has_side_effects=True, vmem_limit_bytes=24 * 2**20
        ),
        name="gather_tiles",
    )(mine)


def reduce_kernel(
    place,
    pieces,
    q,
    terms,
    out,
    own,
    mail,
    sc,
    rc,
    sx,
    rx,
    sy,
    ry,
    sz,
    rz,
    done,
    own_sem,
    mail_sem,
    cs,
    cr,
    xs,
    xr,
    ys,
    yr,
    zs,
    zr,
    keep_sem,
    azs,
    azr,
    ays,
    ayr,
):
    me = place.locate()
    nx, ny, nz = me.nx, me.ny, me.nz
    other = me.at(c=1 - me.c)
    xp, yp, zp = me.x_peers(), me.y_peers(), me.z_peers()
    meet([other] + xp + yp + zp)
    started = []

    def go(copy):
        copy.start()
        started.append(copy)

    def wide(ref):
        return ref[...].astype(jnp.float32)

    def core_copy(p):
        return remote(sc.at[p], rc.at[p], cs.at[p], cr.at[p], other)

    def own_copy(p):
        return pltpu.make_async_copy(terms.at[me.c, p], own.at[p], own_sem.at[p])

    def mail_copy(p):
        return pltpu.make_async_copy(terms.at[1 - me.c, p], mail.at[p], mail_sem.at[p])

    def x_copy(p, k):
        return remote(sx.at[p, k - 1], rx.at[p, k - 1], xs.at[p, k - 1], xr.at[p, k - 1], xp[k - 1])

    def y_copy(p, j):
        return remote(sy.at[p, j - 1], ry.at[p, j - 1], ys.at[p, j - 1], yr.at[p, j - 1], yp[j - 1])

    def z_copy(p, m):
        return remote(sz.at[p, m - 1], rz.at[p, m - 1], zs.at[p, m - 1], zr.at[p, m - 1], zp[m - 1])

    def spread_z(p, m, z):
        return remote(
            done.at[p], out.at[p, me.y, z], azs.at[p, m - 1], azr.at[p, m - 1], zp[m - 1]
        )

    def spread_y(p, j, m, src, y, z):
        return remote(
            src, out.at[p, y, z], ays.at[p, j - 1, m], ayr.at[p, j - 1, m], yp[j - 1]
        )

    def keep_copy(p):
        return pltpu.make_async_copy(done.at[p], out.at[p, me.y, me.z], keep_sem.at[p])

    def fetch(p):
        if p < pieces:
            mail_copy(p).start()
            own_copy(p).start()

    def post(p):
        if p < pieces:
            mail_copy(p).wait()

            def body(n, carry):
                for x in range(nx):
                    sc[p, x, n] = mail[p, x, n].astype(jnp.bfloat16)
                return carry

            lax.fori_loop(0, ny * nz * q, body, 0)
            go(core_copy(p))

    def over_x(p):
        own_copy(p).wait()
        core_copy(p).wait_recv()
        for k in range(1, nx):
            x = me.step_x(k)

            def body(n, carry):
                total = wide(own.at[p, x, n]) + wide(rc.at[p, x, n])
                sx[p, k - 1, n] = total.astype(jnp.bfloat16)
                return carry

            lax.fori_loop(0, ny * nz * q, body, 0)
            go(x_copy(p, k))
        post(p + WINDOW)
        fetch(p + WINDOW + 1)

    def up_to_x(p, n):
        total = wide(own.at[p, me.x, n]) + wide(rc.at[p, me.x, n])
        for k in range(1, nx):
            total = total + wide(rx.at[p, k - 1, n])
        return total

    def up_to_y(p, n):
        total = up_to_x(p, me.y * (nz * q) + n)
        for j in range(1, ny):
            total = total + wide(ry.at[p, j - 1, n])
        return total

    def over_y(p):
        for k in range(1, nx):
            x_copy(p, k).wait_recv()
        for j in range(1, ny):
            first = me.step_y(j) * (nz * q)

            def body(n, carry):
                sy[p, j - 1, n] = up_to_x(p, first + n).astype(jnp.bfloat16)
                return carry

            lax.fori_loop(0, nz * q, body, 0)
            go(y_copy(p, j))

    def over_z(p):
        for j in range(1, ny):
            y_copy(p, j).wait_recv()
        for m in range(1, nz):
            first = me.step_z(m) * q

            def body(i, carry):
                sz[p, m - 1, i] = up_to_y(p, first + i).astype(jnp.bfloat16)
                return carry

            lax.fori_loop(0, q, body, 0)
            go(z_copy(p, m))

    def finish(p):
        for m in range(1, nz):
            z_copy(p, m).wait_recv()

        def body(i, carry):
            total = up_to_y(p, me.z * q + i)
            for m in range(1, nz):
                total = total + wide(rz.at[p, m - 1, i])
            scale = lax.rsqrt(jnp.mean(total * total, keepdims=True) + 1e-06)
            done[p, i] = (total * scale).astype(jnp.bfloat16)
            return carry

        lax.fori_loop(0, q, body, 0)
        for m in range(1, nz):
            go(spread_z(p, m, me.z))
        for j in range(1, ny):
            go(spread_y(p, j, 0, done.at[p], me.y, me.z))
        keep_copy(p).start()

    def pass_on(p):
        for m in range(1, nz):
            z = me.step_z(-m)
            spread_z(p, m, z).wait_recv()
            for j in range(1, ny):
                go(spread_y(p, j, m, out.at[p, me.y, z], me.y, z))

    def collect(p):
        for j in range(1, ny):
            y = me.step_y(-j)
            for m in range(nz):
                z = me.step_z(-m)
                spread_y(p, j, m, done.at[p], y, z).wait_recv()

    for p in range(WINDOW + 1):
        fetch(p)
    for p in range(WINDOW):
        post(p)
    stages = [over_x, over_y, over_z, finish, pass_on, collect]
    for t in range(pieces + len(stages) - 1):
        for s, stage in enumerate(stages):
            if 0 <= t - s < pieces:
                stage(t - s)
    for p in range(pieces):
        keep_copy(p).wait()
    for copy in started:
        copy.wait_send()


def reduce_terms(terms, place, pieces, q):
    side = terms.shape[-1]
    nx, ny, nz = place.nx, place.ny, place.nz
    n = ny * nz * q
    dma = pltpu.SemaphoreType.DMA

    def room(*lead, dtype=jnp.bfloat16):
        return pltpu.VMEM((pieces,) + lead + (side, side), dtype)

    return pl.pallas_call(
        functools.partial(reduce_kernel, place, pieces, q),
        in_specs=[pl.BlockSpec(memory_space=pl.ANY)],
        out_specs=pl.BlockSpec(memory_space=pltpu.VMEM),
        out_shape=jax.ShapeDtypeStruct((pieces, ny, nz, q, side, side), jnp.bfloat16),
        scratch_shapes=[
            room(nx, n, dtype=jnp.float32),
            room(nx, n, dtype=jnp.float32),
            room(nx, n),
            room(nx, n),
            room(nx - 1, n),
            room(nx - 1, n),
            room(ny - 1, nz * q),
            room(ny - 1, nz * q),
            room(nz - 1, q),
            room(nz - 1, q),
            room(q),
            dma((pieces,)),
            dma((pieces,)),
            dma((pieces,)),
            dma((pieces,)),
            dma((pieces, nx - 1)),
            dma((pieces, nx - 1)),
            dma((pieces, ny - 1)),
            dma((pieces, ny - 1)),
            dma((pieces, nz - 1)),
            dma((pieces, nz - 1)),
            dma((pieces,)),
            dma((pieces, nz - 1)),
            dma((pieces, nz - 1)),
            dma((pieces, ny - 1, nz)),
            dma((pieces, ny - 1, nz)),
        ],
        compiler_params=pltpu.CompilerParams(
            collective_id=2, has_side_effects=True, vmem_limit_bytes=48 * 2**20
        ),
        name="reduce_terms",
    )(terms)


def on_device(n_dp, n_fsdp, features, grad_out, weight_tiles, tile_row, tile_column):
    tiles_here, side, _ = weight_tiles.shape
    nblocks = features.shape[1] // side
    place = Place(n_dp, n_fsdp)
    nx, n = place.nx, place.ny * place.nz
    pieces = max(count for count in (1, 2, 4, 8) if tiles_here % (n * count) == 0)
    n = tiles_here // pieces
    blocks, tiles = pattern(tile_row, tile_column, nblocks)
    owner, rest = tiles // tiles_here, tiles % tiles_here
    places = ((owner % 2 * pieces + rest // n) * nx + owner // 2) * n + rest % n
    whole = gather_tiles(weight_tiles, place)
    grad_features, partial = layer(features, grad_out, whole, blocks, tiles, places)
    terms = partial.reshape(2, pieces, nx, n, side, side)
    tile_update = reduce_terms(terms, place, pieces, n // (place.ny * place.nz))
    return (grad_features, tile_update.reshape(tiles_here, side, side).astype(jnp.float32))


def solution(mesh):
    return jax.shard_map(
        functools.partial(on_device, mesh.shape["dp"], mesh.shape["fsdp"]),
        mesh=mesh,
        in_specs=(
            P(("dp", "fsdp"), None),
            P(("dp", "fsdp"), None),
            P("fsdp", None, None),
            P(),
            P(),
        ),
        out_specs=(P(("dp", "fsdp"), None), P("fsdp", None, None)),
        check_vma=False,
    )
```

```python
import functools
import math

import jax
import jax.numpy as jnp
from jax import lax
from jax.experimental import pallas as pl
from jax.experimental.pallas import tpu as pltpu
from jax.sharding import PartitionSpec as P

SIDE_BLOCKS = 4
MESH = pl.DeviceIdType.MESH
WINDOW = 3
ROOT = math.sqrt(2.0 / math.pi)


def gelu_slope(value):
    square = value * value
    half = 0.5 + 0.5 * jnp.tanh(value * (ROOT + (0.044715 * ROOT) * square))
    return half + half * (1.0 - half) * (value * (2.0 * ROOT + (6.0 * 0.044715 * ROOT) * square))


def pattern(tile_row, tile_column, nblocks, tiles_here, run, nx):
    total = tile_row.shape[1]
    f32, i32 = jnp.float32, jnp.int32
    mask = jnp.max(jnp.bitwise_xor(tile_row, tile_column).astype(f32), axis=1, keepdims=True)
    mask = mask.astype(i32)

    def key(block):
        inside = jnp.bitwise_and(block, jnp.broadcast_to(mask, block.shape))
        return ((block - inside) * nblocks + inside).astype(f32)

    def place(block):
        count = block.shape[1]
        keys = key(lax.broadcasted_iota(i32, (nblocks, count), 0))
        below = jnp.where(keys < key(block), 1.0, 0.0)
        return jnp.sum(below, axis=0, keepdims=True)

    def inverse(values):
        count = values.shape[1]
        down = lax.broadcasted_iota(i32, (count, count), 0).astype(f32)
        along = lax.broadcasted_iota(i32, (count, count), 1).astype(f32)
        column = jnp.sum(jnp.where(down == along, values, 0.0), axis=1, keepdims=True)
        return jnp.sum(jnp.where(column == along, down, 0.0), axis=0, keepdims=True)

    def divide(value, by):
        whole = jnp.floor((value + 0.5) * (1.0 / by))
        return whole, value - whole * by

    blocks = inverse(place(lax.broadcasted_iota(i32, (1, nblocks), 1)))
    at_row, at_column = place(tile_row), place(tile_column)
    tiles = inverse(at_column * SIDE_BLOCKS + divide(at_row, SIDE_BLOCKS)[1])
    owner, rest = divide(tiles, tiles_here)
    x, core = divide(owner, 2)
    piece, left = divide(rest, run)
    places = ((core * (tiles_here // run) + piece) * nx + x) * run + left
    return blocks.astype(i32), tiles.astype(i32), places.astype(i32)


def layer_kernel(steps, blocks, tiles, places, features, grads, whole, out_ref, partial_ref, term_buf, sems):
    n, m = SIDE_BLOCKS, SIDE_BLOCKS * SIDE_BLOCKS
    side = whole.shape[1]

    def drain(slot):
        pltpu.make_async_copy(
            term_buf.at[slot], partial_ref.at[pl.ds(0, m)], sems.at[slot]
        ).wait()

    def group(g, slot):
        columns = [
            pl.ds(pl.multiple_of(blocks[0, g * n + k] * side, side), side) for k in range(n)
        ]
        feature = jnp.concatenate([features[:, at] for at in columns], axis=1)
        grad = jnp.concatenate([grads[:, at] for at in columns], axis=1).astype(jnp.float32)
        weight = jnp.concatenate(
            [
                jnp.concatenate([whole[tiles[0, g * m + c * n + r]] for r in range(n)], axis=1)
                for c in range(n)
            ],
            axis=0,
        )
        preact = jnp.dot(feature, weight, preferred_element_type=jnp.float32)
        slope = (grad * gelu_slope(preact)).astype(jnp.bfloat16)
        back = lax.dot_general(
            slope, weight, (((1,), (1,)), ((), ())), preferred_element_type=jnp.float32
        )
        result = (grad + back).astype(jnp.bfloat16)
        for k, at in enumerate(columns):
            out_ref[:, at] = result[:, k * side : (k + 1) * side]
        term = lax.dot_general(
            feature, slope, (((0,), (0,)), ((), ())), preferred_element_type=jnp.float32
        )
        for c in range(n):
            for r in range(n):
                term_buf[slot, c * n + r] = term[
                    c * side : (c + 1) * side, r * side : (r + 1) * side
                ]
        for k in range(m):
            pltpu.make_async_copy(
                term_buf.at[slot, k], partial_ref.at[places[0, g * m + k]], sems.at[slot]
            ).start()

    slots = term_buf.shape[0]

    def body(i, carry):
        for k in range(slots):

            @pl.when(i > 0)
            def _():
                drain(k)

            group(i * slots + k, k)
        return carry

    lax.fori_loop(0, steps // slots, body, 0)
    for k in range(slots):
        drain(k)


def layer(features, grad_out, whole, blocks, tiles, places):
    rows, width = features.shape
    total, side, _ = whole.shape
    n, m = SIDE_BLOCKS, SIDE_BLOCKS * SIDE_BLOCKS
    steps = width // side // n
    slots = 2 if steps % 2 == 0 else 1
    vmem = pl.BlockSpec(memory_space=pltpu.VMEM)
    smem = pl.BlockSpec(memory_space=pltpu.SMEM)
    return pl.pallas_call(
        functools.partial(layer_kernel, steps),
        in_specs=[smem] * 3 + [vmem] * 3,
        out_specs=[vmem, pl.BlockSpec(memory_space=pl.ANY)],
        scratch_shapes=[
            pltpu.VMEM((slots, m, side, side), jnp.float32),
            pltpu.SemaphoreType.DMA((slots,)),
        ],
        out_shape=[
            jax.ShapeDtypeStruct((rows, width), jnp.bfloat16),
            jax.ShapeDtypeStruct((total, side, side), jnp.float32),
        ],
        compiler_params=pltpu.CompilerParams(vmem_limit_bytes=26 * 2**20),
        cost_estimate=pl.CostEstimate(
            flops=6 * rows * width * n * side,
            bytes_accessed=6 * rows * width + 6 * total * side * side,
            transcendentals=rows * width,
        ),
        name="layer",
    )(blocks, tiles, places, features, grad_out, whole)


class Place:
    def __init__(self, n_dp, n_fsdp):
        self.cores = 2
        self.nx = n_fsdp // 2
        self.ny = 2 if n_dp <= 8 else 4
        self.nz = n_dp // self.ny

    def locate(self):
        fsdp, dp = lax.axis_index("fsdp"), lax.axis_index("dp")
        self.x, self.c = fsdp // 2, fsdp % 2
        self.z, self.y = dp // self.ny, dp % self.ny
        return self

    def at(self, x=None, c=None, y=None, z=None):
        x = self.x if x is None else x
        c = self.c if c is None else c
        y = self.y if y is None else y
        z = self.z if z is None else z
        return (z * self.ny + y, x * 2 + c)

    def step_x(self, k):
        return lax.rem(self.x + k + self.nx, self.nx)

    def step_y(self, k):
        return lax.rem(self.y + k + self.ny, self.ny)

    def step_z(self, k):
        return lax.rem(self.z + k + self.nz, self.nz)

    def x_peers(self):
        return [self.at(x=self.step_x(k)) for k in range(1, self.nx)]

    def y_peers(self):
        return [self.at(y=self.step_y(k)) for k in range(1, self.ny)]

    def z_peers(self):
        return [self.at(z=self.step_z(k)) for k in range(1, self.nz)]


def meet(peers):
    barrier = pltpu.get_barrier_semaphore()
    for peer in peers:
        pl.semaphore_signal(barrier, inc=1, device_id=peer, device_id_type=MESH)
    pl.semaphore_wait(barrier, len(peers))


def remote(src, dst, send, recv, peer):
    return pltpu.make_async_remote_copy(
        src_ref=src, dst_ref=dst, send_sem=send, recv_sem=recv, device_id=peer, device_id_type=MESH
    )


def gather_kernel(
    place, nw, pieces, find, mine, row, column, whole, blocks, order, places,
    own_sem, xs, xr, ys, yr, zs, zr, ds, dr, cs, cr, ws, wr
):
    me = place.locate()
    nx, ny = me.nx, me.ny
    tiles = mine.shape[0]
    part = tiles // (ny * nw)
    q = part // pieces
    w = me.z % nw
    other = me.at(c=1 - me.c)
    xp, yp = me.x_peers(), me.y_peers()
    zp = me.at(z=me.z + 1 - 2 * w) if nw == 2 else None
    meet(xp + yp + [other] + ([zp] if nw == 2 else []))
    run = ny * nw * q
    started = []

    def go(copy):
        copy.start()
        started.append(copy)

    def inner(y, v, p):
        return y * (nw * part) + v * part + p * q

    def span(x, y, v, p, core=None):
        core = me.c if core is None else core
        return whole.at[pl.ds((x * 2 + core) * tiles + inner(y, v, p), q)]

    def x_copy(p, k, x):
        return remote(
            mine.at[pl.ds(inner(me.y, w, p), q)],
            span(x, me.y, w, p),
            xs.at[k - 1, p],
            xr.at[k - 1, p],
            xp[k - 1],
        )

    def home(core, p):
        return whole.at[pl.ds((me.x * 2 + core) * tiles + p * run, run)]

    def own_copy(p):
        return pltpu.make_async_copy(mine.at[pl.ds(p * run, run)], home(me.c, p), own_sem.at[p])

    def core_copy(p, core):
        return remote(mine.at[pl.ds(p * run, run)], home(core, p), ws.at[p], wr.at[p], other)

    def in_chip(k, j, v, p, at):
        return remote(at, at, cs.at[k - 1, j, v, p], cr.at[k - 1, j, v, p], other)

    def y_copy(k, j, y, p):
        at = span(me.step_x(-k), y, w, p)
        return remote(at, at, ys.at[k - 1, j - 1, p], yr.at[k - 1, j - 1, p], yp[j - 1])

    def z_copy(k, v, p):
        at = span(me.step_x(-k), me.y, v, p)
        return remote(at, at, zs.at[k - 1, p], zr.at[k - 1, p], zp)

    def last_copy(k, j, y, v, p):
        at = span(me.step_x(-k), y, v, p)
        peer = zp if p % 2 == 0 else yp[j - 1]
        return remote(at, at, ds.at[k - 1, j - 1, p], dr.at[k - 1, j - 1, p], peer)

    def land_x(p):
        for k in range(1, nx):
            x = me.step_x(-k)
            x_copy(p, k, x).wait_recv()
            for j in range(1, ny):
                go(y_copy(k, j, me.y, p))
            if nw == 2:
                go(z_copy(k, w, p))
            go(in_chip(k, 0, 0, p, span(x, me.y, w, p)))
            x_copy(p, k, me.x).wait_send()
            if p + WINDOW < pieces:
                x_copy(p + WINDOW, k, me.x).start()
        go(core_copy(p, me.c))
        own_copy(p).start()

    def land_yz(p):
        for k in range(1, nx):
            x = me.step_x(-k)
            for j in range(1, ny):
                y = me.step_y(-j)
                y_copy(k, j, y, p).wait_recv()
                if nw == 2 and p % 2 == 0:
                    go(last_copy(k, j, y, w, p))
                go(in_chip(k, j, 0, p, span(x, y, w, p)))
            if nw == 2:
                z_copy(k, 1 - w, p).wait_recv()
                if p % 2 == 1:
                    for j in range(1, ny):
                        go(last_copy(k, j, me.y, 1 - w, p))
                go(in_chip(k, 0, 1, p, span(x, me.y, 1 - w, p)))

    def land_last(p):
        for k in range(1, nx):
            x = me.step_x(-k)
            for j in range(1, ny):
                y = me.step_y(-j)
                last_copy(k, j, y, 1 - w, p).wait_recv()
                go(in_chip(k, j, 1, p, span(x, y, 1 - w, p)))

    for p in range(min(WINDOW, pieces)):
        for k in range(1, nx):
            x_copy(p, k, me.x).start()
    blocks[...], order[...], places[...] = find(row[...], column[...])
    stages = [land_x, land_yz] + ([land_last] if nw == 2 else [])
    for t in range(pieces + len(stages) - 1):
        for s, stage in enumerate(stages):
            if 0 <= t - s < pieces:
                stage(t - s)
    for p in range(pieces):
        own_copy(p).wait()
        core_copy(p, 1 - me.c).wait_recv()
        for k in range(1, nx):
            x = me.step_x(-k)
            for j in range(ny):
                y = me.step_y(-j)
                for v in range(nw):
                    u = w if v == 0 else 1 - w
                    in_chip(k, j, v, p, span(x, y, u, p, 1 - me.c)).wait_recv()
    for copy in started:
        copy.wait_send()


def gather_tiles(mine, tile_row, tile_column, nblocks, run, place):
    tiles, side, _ = mine.shape
    nx, ny = place.nx, place.ny
    nw = 2 if place.nz % 2 == 0 and tiles % (2 * ny) == 0 else 1
    part = tiles // (ny * nw)
    pieces = 4 if part % 4 == 0 else 1
    total = tiles * nx * 2
    find = functools.partial(pattern, nblocks=nblocks, tiles_here=tiles, run=run, nx=nx)
    vmem = pl.BlockSpec(memory_space=pltpu.VMEM)
    dma = pltpu.SemaphoreType.DMA
    return pl.pallas_call(
        functools.partial(gather_kernel, place, nw, pieces, find),
        in_specs=[vmem] * 3,
        out_specs=[vmem] * 4,
        out_shape=[
            jax.ShapeDtypeStruct((total, side, side), mine.dtype),
            jax.ShapeDtypeStruct((1, nblocks), jnp.int32),
            jax.ShapeDtypeStruct((1, total), jnp.int32),
            jax.ShapeDtypeStruct((1, total), jnp.int32),
        ],
        scratch_shapes=[dma((pieces,))]
        + [dma((nx - 1, pieces))] * 2
        + [dma((nx - 1, ny - 1, pieces))] * 2
        + [dma((nx - 1, pieces))] * 2
        + [dma((nx - 1, ny - 1, pieces))] * 2
        + [dma((nx - 1, ny, nw, pieces))] * 2
        + [dma((pieces,))] * 2,
        compiler_params=pltpu.CompilerParams(
            collective_id=1, has_side_effects=True, vmem_limit_bytes=24 * 2**20
        ),
        name="gather_tiles",
    )(mine, tile_row.reshape(1, total), tile_column.reshape(1, total))


def reduce_kernel(
    place,
    pieces,
    q,
    terms,
    out,
    own,
    mail,
    sc,
    rc,
    sx,
    rx,
    sy,
    ry,
    sz,
    rz,
    done,
    own_sem,
    mail_sem,
    cs,
    cr,
    xs,
    xr,
    ys,
    yr,
    zs,
    zr,
    keep_sem,
    azs,
    azr,
    ays,
    ayr,
):
    me = place.locate()
    nx, ny, nz = me.nx, me.ny, me.nz
    other = me.at(c=1 - me.c)
    xp, yp, zp = me.x_peers(), me.y_peers(), me.z_peers()
    meet([other] + xp + yp + zp)
    started = []

    def go(copy):
        copy.start()
        started.append(copy)

    def wide(ref):
        return ref[...].astype(jnp.float32)

    def core_copy(p):
        return remote(sc.at[p], rc.at[p], cs.at[p], cr.at[p], other)

    def own_copy(p):
        return pltpu.make_async_copy(terms.at[me.c, p], own.at[p], own_sem.at[p])

    def mail_copy(p):
        return pltpu.make_async_copy(terms.at[1 - me.c, p], mail.at[p], mail_sem.at[p])

    def x_copy(p, k):
        return remote(sx.at[p, k - 1], rx.at[p, k - 1], xs.at[p, k - 1], xr.at[p, k - 1], xp[k - 1])

    def y_copy(p, j):
        return remote(sy.at[p, j - 1], ry.at[p, j - 1], ys.at[p, j - 1], yr.at[p, j - 1], yp[j - 1])

    def z_copy(p, m):
        return remote(sz.at[p, m - 1], rz.at[p, m - 1], zs.at[p, m - 1], zr.at[p, m - 1], zp[m - 1])

    def spread_z(p, m, z):
        return remote(
            done.at[p], out.at[p, me.y, z], azs.at[p, m - 1], azr.at[p, m - 1], zp[m - 1]
        )

    def spread_y(p, j, m, src, y, z):
        return remote(
            src, out.at[p, y, z], ays.at[p, j - 1, m], ayr.at[p, j - 1, m], yp[j - 1]
        )

    def keep_copy(p):
        return pltpu.make_async_copy(done.at[p], out.at[p, me.y, me.z], keep_sem.at[p])

    def fetch(p):
        if p < pieces:
            mail_copy(p).start()
            own_copy(p).start()

    def post(p):
        if p < pieces:
            mail_copy(p).wait()

            def body(n, carry):
                for x in range(nx):
                    sc[p, x, n] = mail[p, x, n].astype(jnp.bfloat16)
                return carry

            lax.fori_loop(0, ny * nz * q, body, 0)
            go(core_copy(p))

    def over_x(p):
        own_copy(p).wait()
        core_copy(p).wait_recv()
        for k in range(1, nx):
            x = me.step_x(k)

            def body(n, carry):
                total = wide(own.at[p, x, n]) + wide(rc.at[p, x, n])
                sx[p, k - 1, n] = total.astype(jnp.bfloat16)
                return carry

            lax.fori_loop(0, ny * nz * q, body, 0)
            go(x_copy(p, k))
        post(p + WINDOW)
        fetch(p + WINDOW + 1)

    def up_to_x(p, n):
        total = wide(own.at[p, me.x, n]) + wide(rc.at[p, me.x, n])
        for k in range(1, nx):
            total = total + wide(rx.at[p, k - 1, n])
        return total

    def up_to_y(p, n):
        total = up_to_x(p, me.y * (nz * q) + n)
        for j in range(1, ny):
            total = total + wide(ry.at[p, j - 1, n])
        return total

    def over_y(p):
        for k in range(1, nx):
            x_copy(p, k).wait_recv()
        for j in range(1, ny):
            first = me.step_y(j) * (nz * q)

            def body(n, carry):
                sy[p, j - 1, n] = up_to_x(p, first + n).astype(jnp.bfloat16)
                return carry

            lax.fori_loop(0, nz * q, body, 0)
            go(y_copy(p, j))

    def over_z(p):
        for j in range(1, ny):
            y_copy(p, j).wait_recv()
        for m in range(1, nz):
            first = me.step_z(m) * q

            def body(i, carry):
                sz[p, m - 1, i] = up_to_y(p, first + i).astype(jnp.bfloat16)
                return carry

            lax.fori_loop(0, q, body, 0)
            go(z_copy(p, m))

    def finish(p):
        for m in range(1, nz):
            z_copy(p, m).wait_recv()

        def body(i, carry):
            total = up_to_y(p, me.z * q + i)
            for m in range(1, nz):
                total = total + wide(rz.at[p, m - 1, i])
            scale = lax.rsqrt(jnp.mean(total * total, keepdims=True) + 1e-06)
            done[p, i] = (total * scale).astype(jnp.bfloat16)
            return carry

        lax.fori_loop(0, q, body, 0)
        for m in range(1, nz):
            go(spread_z(p, m, me.z))
        for j in range(1, ny):
            go(spread_y(p, j, 0, done.at[p], me.y, me.z))
        keep_copy(p).start()

    def pass_on(p):
        for m in range(1, nz):
            z = me.step_z(-m)
            spread_z(p, m, z).wait_recv()
            for j in range(1, ny):
                go(spread_y(p, j, m, out.at[p, me.y, z], me.y, z))

    def collect(p):
        for j in range(1, ny):
            y = me.step_y(-j)
            for m in range(nz):
                z = me.step_z(-m)
                spread_y(p, j, m, done.at[p], y, z).wait_recv()

    for p in range(WINDOW + 1):
        fetch(p)
    for p in range(WINDOW):
        post(p)
    stages = [over_x, over_y, over_z, finish, pass_on, collect]
    lags = [0] + list(range(2, len(stages) + 1))
    for t in range(pieces + lags[-1]):
        for lag, stage in zip(lags, stages):
            if 0 <= t - lag < pieces:
                stage(t - lag)
    for p in range(pieces):
        keep_copy(p).wait()
    for copy in started:
        copy.wait_send()


def reduce_terms(terms, place, pieces, q):
    side = terms.shape[-1]
    nx, ny, nz = place.nx, place.ny, place.nz
    n = ny * nz * q
    dma = pltpu.SemaphoreType.DMA

    def room(*lead, dtype=jnp.bfloat16):
        return pltpu.VMEM((pieces,) + lead + (side, side), dtype)

    return pl.pallas_call(
        functools.partial(reduce_kernel, place, pieces, q),
        in_specs=[pl.BlockSpec(memory_space=pl.ANY)],
        out_specs=pl.BlockSpec(memory_space=pltpu.VMEM),
        out_shape=jax.ShapeDtypeStruct((pieces, ny, nz, q, side, side), jnp.bfloat16),
        scratch_shapes=[
            room(nx, n, dtype=jnp.float32),
            room(nx, n, dtype=jnp.float32),
            room(nx, n),
            room(nx, n),
            room(nx - 1, n),
            room(nx - 1, n),
            room(ny - 1, nz * q),
            room(ny - 1, nz * q),
            room(nz - 1, q),
            room(nz - 1, q),
            room(q),
            dma((pieces,)),
            dma((pieces,)),
            dma((pieces,)),
            dma((pieces,)),
            dma((pieces, nx - 1)),
            dma((pieces, nx - 1)),
            dma((pieces, ny - 1)),
            dma((pieces, ny - 1)),
            dma((pieces, nz - 1)),
            dma((pieces, nz - 1)),
            dma((pieces,)),
            dma((pieces, nz - 1)),
            dma((pieces, nz - 1)),
            dma((pieces, ny - 1, nz)),
            dma((pieces, ny - 1, nz)),
        ],
        compiler_params=pltpu.CompilerParams(
            collective_id=2, has_side_effects=True, vmem_limit_bytes=48 * 2**20
        ),
        name="reduce_terms",
    )(terms)


def on_device(n_dp, n_fsdp, features, grad_out, weight_tiles, tile_row, tile_column):
    tiles_here, side, _ = weight_tiles.shape
    nblocks = features.shape[1] // side
    place = Place(n_dp, n_fsdp)
    nx, n = place.nx, place.ny * place.nz
    pieces = max(count for count in (1, 2, 4, 8) if tiles_here % (n * count) == 0)
    n = tiles_here // pieces
    whole, blocks, tiles, places = gather_tiles(
        weight_tiles, tile_row, tile_column, nblocks, n, place
    )
    grad_features, partial = layer(features, grad_out, whole, blocks, tiles, places)
    terms = partial.reshape(2, pieces, nx, n, side, side)
    tile_update = reduce_terms(terms, place, pieces, n // (place.ny * place.nz))
    return (grad_features, tile_update.reshape(tiles_here, side, side).astype(jnp.float32))


def solution(mesh):
    return jax.shard_map(
        functools.partial(on_device, mesh.shape["dp"], mesh.shape["fsdp"]),
        mesh=mesh,
        in_specs=(
            P(("dp", "fsdp"), None),
            P(("dp", "fsdp"), None),
            P("fsdp", None, None),
            P(),
            P(),
        ),
        out_specs=(P(("dp", "fsdp"), None), P("fsdp", None, None)),
        check_vma=False,
    )
```

```python
import functools
import math

import jax
import jax.numpy as jnp
from jax import lax
from jax.experimental import pallas as pl
from jax.experimental.pallas import tpu as pltpu
from jax.sharding import PartitionSpec as P

SIDE_BLOCKS = 4
MESH = pl.DeviceIdType.MESH
WINDOW = 3
ROOT = math.sqrt(2.0 / math.pi)


def gelu_slope(value):
    square = value * value
    half = 0.5 + 0.5 * jnp.tanh(value * (ROOT + (0.044715 * ROOT) * square))
    return half + half * (1.0 - half) * (value * (2.0 * ROOT + (6.0 * 0.044715 * ROOT) * square))


def pattern(tile_row, tile_column, nblocks, tiles_here, run, nx):
    total = tile_row.shape[1]
    f32, i32 = jnp.float32, jnp.int32
    mask = jnp.max(jnp.bitwise_xor(tile_row, tile_column).astype(f32), axis=1, keepdims=True)
    mask = mask.astype(i32)

    def key(block):
        inside = jnp.bitwise_and(block, jnp.broadcast_to(mask, block.shape))
        return ((block - inside) * nblocks + inside).astype(f32)

    def place(block):
        count = block.shape[1]
        keys = key(lax.broadcasted_iota(i32, (nblocks, count), 0))
        below = jnp.where(keys < key(block), 1.0, 0.0)
        return jnp.sum(below, axis=0, keepdims=True)

    def inverse(values):
        count = values.shape[1]
        down = lax.broadcasted_iota(i32, (count, count), 0).astype(f32)
        along = lax.broadcasted_iota(i32, (count, count), 1).astype(f32)
        column = jnp.sum(jnp.where(down == along, values, 0.0), axis=1, keepdims=True)
        return jnp.sum(jnp.where(column == along, down, 0.0), axis=0, keepdims=True)

    def divide(value, by):
        whole = jnp.floor((value + 0.5) * (1.0 / by))
        return whole, value - whole * by

    blocks = inverse(place(lax.broadcasted_iota(i32, (1, nblocks), 1)))
    at_row, at_column = place(tile_row), place(tile_column)
    tiles = inverse(at_column * SIDE_BLOCKS + divide(at_row, SIDE_BLOCKS)[1])
    owner, rest = divide(tiles, tiles_here)
    x, core = divide(owner, 2)
    piece, left = divide(rest, run)
    places = ((core * (tiles_here // run) + piece) * nx + x) * run + left
    return blocks.astype(i32), tiles.astype(i32), places.astype(i32)


def layer_kernel(steps, blocks, tiles, places, features, grads, whole, out_ref, partial_ref, term_buf, sems):
    n, m = SIDE_BLOCKS, SIDE_BLOCKS * SIDE_BLOCKS
    side = whole.shape[1]

    def drain(slot):
        pltpu.make_async_copy(
            term_buf.at[slot], partial_ref.at[pl.ds(0, m)], sems.at[slot]
        ).wait()

    def group(g, slot):
        columns = [
            pl.ds(pl.multiple_of(blocks[0, g * n + k] * side, side), side) for k in range(n)
        ]
        feature = jnp.concatenate([features[:, at] for at in columns], axis=1)
        grad = jnp.concatenate([grads[:, at] for at in columns], axis=1).astype(jnp.float32)
        weight = jnp.concatenate(
            [
                jnp.concatenate([whole[tiles[0, g * m + c * n + r]] for r in range(n)], axis=1)
                for c in range(n)
            ],
            axis=0,
        )
        preact = jnp.dot(feature, weight, preferred_element_type=jnp.float32)
        slope = (grad * gelu_slope(preact)).astype(jnp.bfloat16)
        back = lax.dot_general(
            slope, weight, (((1,), (1,)), ((), ())), preferred_element_type=jnp.float32
        )
        result = (grad + back).astype(jnp.bfloat16)
        for k, at in enumerate(columns):
            out_ref[:, at] = result[:, k * side : (k + 1) * side]
        term = lax.dot_general(
            feature, slope, (((0,), (0,)), ((), ())), preferred_element_type=jnp.float32
        )
        for c in range(n):
            for r in range(n):
                term_buf[slot, c * n + r] = term[
                    c * side : (c + 1) * side, r * side : (r + 1) * side
                ]
        for k in range(m):
            pltpu.make_async_copy(
                term_buf.at[slot, k], partial_ref.at[places[0, g * m + k]], sems.at[slot]
            ).start()

    slots = term_buf.shape[0]

    def body(i, carry):
        for k in range(slots):

            @pl.when(i > 0)
            def _():
                drain(k)

            group(i * slots + k, k)
        return carry

    lax.fori_loop(0, steps // slots, body, 0)
    for k in range(slots):
        drain(k)


def layer(features, grad_out, whole, blocks, tiles, places):
    rows, width = features.shape
    total, side, _ = whole.shape
    n, m = SIDE_BLOCKS, SIDE_BLOCKS * SIDE_BLOCKS
    steps = width // side // n
    slots = 2 if steps % 2 == 0 else 1
    vmem = pl.BlockSpec(memory_space=pltpu.VMEM)
    smem = pl.BlockSpec(memory_space=pltpu.SMEM)
    return pl.pallas_call(
        functools.partial(layer_kernel, steps),
        in_specs=[smem] * 3 + [vmem] * 3,
        out_specs=[vmem, pl.BlockSpec(memory_space=pl.ANY)],
        scratch_shapes=[
            pltpu.VMEM((slots, m, side, side), jnp.float32),
            pltpu.SemaphoreType.DMA((slots,)),
        ],
        out_shape=[
            jax.ShapeDtypeStruct((rows, width), jnp.bfloat16),
            jax.ShapeDtypeStruct((total, side, side), jnp.float32),
        ],
        compiler_params=pltpu.CompilerParams(vmem_limit_bytes=26 * 2**20),
        cost_estimate=pl.CostEstimate(
            flops=6 * rows * width * n * side,
            bytes_accessed=6 * rows * width + 6 * total * side * side,
            transcendentals=rows * width,
        ),
        name="layer",
    )(blocks, tiles, places, features, grad_out, whole)


class Place:
    def __init__(self, n_dp, n_fsdp):
        self.cores = 2
        self.nx = n_fsdp // 2
        self.ny = 2 if n_dp <= 8 else 4
        self.nz = n_dp // self.ny

    def locate(self):
        fsdp, dp = lax.axis_index("fsdp"), lax.axis_index("dp")
        self.x, self.c = fsdp // 2, fsdp % 2
        self.z, self.y = dp // self.ny, dp % self.ny
        return self

    def at(self, x=None, c=None, y=None, z=None):
        x = self.x if x is None else x
        c = self.c if c is None else c
        y = self.y if y is None else y
        z = self.z if z is None else z
        return (z * self.ny + y, x * 2 + c)

    def step_x(self, k):
        return lax.rem(self.x + k + self.nx, self.nx)

    def step_y(self, k):
        return lax.rem(self.y + k + self.ny, self.ny)

    def step_z(self, k):
        return lax.rem(self.z + k + self.nz, self.nz)

    def x_peers(self):
        return [self.at(x=self.step_x(k)) for k in range(1, self.nx)]

    def y_peers(self):
        return [self.at(y=self.step_y(k)) for k in range(1, self.ny)]

    def z_peers(self):
        return [self.at(z=self.step_z(k)) for k in range(1, self.nz)]


def meet(peers):
    barrier = pltpu.get_barrier_semaphore()
    for peer in peers:
        pl.semaphore_signal(barrier, inc=1, device_id=peer, device_id_type=MESH)
    pl.semaphore_wait(barrier, len(peers))


def remote(src, dst, send, recv, peer):
    return pltpu.make_async_remote_copy(
        src_ref=src, dst_ref=dst, send_sem=send, recv_sem=recv, device_id=peer, device_id_type=MESH
    )


def gather_kernel(
    place, nw, pieces, find, mine, row, column, features, grads,
    whole, blocks, order, places, features_here, grads_here, rows_sem, own_sem, xs, xr, ys, yr, zs, zr, ds, dr, cs, cr, ws, wr
):
    me = place.locate()
    nx, ny = me.nx, me.ny
    tiles = mine.shape[0]
    part = tiles // (ny * nw)
    q = part // pieces
    w = me.z % nw
    other = me.at(c=1 - me.c)
    xp, yp = me.x_peers(), me.y_peers()
    zp = me.at(z=me.z + 1 - 2 * w) if nw == 2 else None
    loads = [
        pltpu.make_async_copy(features, features_here, rows_sem.at[0]),
        pltpu.make_async_copy(grads, grads_here, rows_sem.at[1]),
    ]
    meet(xp + yp + [other] + ([zp] if nw == 2 else []))
    run = ny * nw * q
    started = []

    def go(copy):
        copy.start()
        started.append(copy)

    def inner(y, v, p):
        return y * (nw * part) + v * part + p * q

    def span(x, y, v, p, core=None):
        core = me.c if core is None else core
        return whole.at[pl.ds((x * 2 + core) * tiles + inner(y, v, p), q)]

    def x_copy(p, k, x):
        return remote(
            mine.at[pl.ds(inner(me.y, w, p), q)],
            span(x, me.y, w, p),
            xs.at[k - 1, p],
            xr.at[k - 1, p],
            xp[k - 1],
        )

    def home(core, p):
        return whole.at[pl.ds((me.x * 2 + core) * tiles + p * run, run)]

    def own_copy(p):
        return pltpu.make_async_copy(mine.at[pl.ds(p * run, run)], home(me.c, p), own_sem.at[p])

    def core_copy(p, core):
        return remote(mine.at[pl.ds(p * run, run)], home(core, p), ws.at[p], wr.at[p], other)

    def in_chip(k, j, v, p, at):
        return remote(at, at, cs.at[k - 1, j, v, p], cr.at[k - 1, j, v, p], other)

    def y_copy(k, j, y, p):
        at = span(me.step_x(-k), y, w, p)
        return remote(at, at, ys.at[k - 1, j - 1, p], yr.at[k - 1, j - 1, p], yp[j - 1])

    def z_copy(k, v, p):
        at = span(me.step_x(-k), me.y, v, p)
        return remote(at, at, zs.at[k - 1, p], zr.at[k - 1, p], zp)

    def last_copy(k, j, y, v, p):
        at = span(me.step_x(-k), y, v, p)
        peer = zp if p % 2 == 0 else yp[j - 1]
        return remote(at, at, ds.at[k - 1, j - 1, p], dr.at[k - 1, j - 1, p], peer)

    def land_x(p):
        for k in range(1, nx):
            x = me.step_x(-k)
            x_copy(p, k, x).wait_recv()
            for j in range(1, ny):
                go(y_copy(k, j, me.y, p))
            if nw == 2:
                go(z_copy(k, w, p))
            go(in_chip(k, 0, 0, p, span(x, me.y, w, p)))
            x_copy(p, k, me.x).wait_send()
            if p + WINDOW < pieces:
                x_copy(p + WINDOW, k, me.x).start()
        go(core_copy(p, me.c))
        own_copy(p).start()

    def land_yz(p):
        for k in range(1, nx):
            x = me.step_x(-k)
            for j in range(1, ny):
                y = me.step_y(-j)
                y_copy(k, j, y, p).wait_recv()
                if nw == 2 and p % 2 == 0:
                    go(last_copy(k, j, y, w, p))
                go(in_chip(k, j, 0, p, span(x, y, w, p)))
            if nw == 2:
                z_copy(k, 1 - w, p).wait_recv()
                if p % 2 == 1:
                    for j in range(1, ny):
                        go(last_copy(k, j, me.y, 1 - w, p))
                go(in_chip(k, 0, 1, p, span(x, me.y, 1 - w, p)))

    def land_last(p):
        for k in range(1, nx):
            x = me.step_x(-k)
            for j in range(1, ny):
                y = me.step_y(-j)
                last_copy(k, j, y, 1 - w, p).wait_recv()
                go(in_chip(k, j, 1, p, span(x, y, 1 - w, p)))

    for p in range(min(WINDOW, pieces)):
        for k in range(1, nx):
            x_copy(p, k, me.x).start()
    for load in loads:
        load.start()
    blocks[...], order[...], places[...] = find(row[...], column[...])
    stages = [land_x, land_yz] + ([land_last] if nw == 2 else [])
    for t in range(pieces + len(stages) - 1):
        for s, stage in enumerate(stages):
            if 0 <= t - s < pieces:
                stage(t - s)
    for p in range(pieces):
        own_copy(p).wait()
        core_copy(p, 1 - me.c).wait_recv()
        for k in range(1, nx):
            x = me.step_x(-k)
            for j in range(ny):
                y = me.step_y(-j)
                for v in range(nw):
                    u = w if v == 0 else 1 - w
                    in_chip(k, j, v, p, span(x, y, u, p, 1 - me.c)).wait_recv()
    for load in loads:
        load.wait()
    for copy in started:
        copy.wait_send()


def gather_tiles(mine, tile_row, tile_column, features, grad_out, nblocks, run, place):
    tiles, side, _ = mine.shape
    nx, ny = place.nx, place.ny
    nw = 2 if place.nz % 2 == 0 and tiles % (2 * ny) == 0 else 1
    part = tiles // (ny * nw)
    pieces = 4 if part % 4 == 0 else 1
    total = tiles * nx * 2
    find = functools.partial(pattern, nblocks=nblocks, tiles_here=tiles, run=run, nx=nx)
    vmem = pl.BlockSpec(memory_space=pltpu.VMEM)
    dma = pltpu.SemaphoreType.DMA
    return pl.pallas_call(
        functools.partial(gather_kernel, place, nw, pieces, find),
        in_specs=[vmem] * 3 + [pl.BlockSpec(memory_space=pl.ANY)] * 2,
        out_specs=[vmem] * 6,
        out_shape=[
            jax.ShapeDtypeStruct((total, side, side), mine.dtype),
            jax.ShapeDtypeStruct((1, nblocks), jnp.int32),
            jax.ShapeDtypeStruct((1, total), jnp.int32),
            jax.ShapeDtypeStruct((1, total), jnp.int32),
            jax.ShapeDtypeStruct(features.shape, features.dtype),
            jax.ShapeDtypeStruct(grad_out.shape, grad_out.dtype),
        ],
        scratch_shapes=[dma((2,)), dma((pieces,))]
        + [dma((nx - 1, pieces))] * 2
        + [dma((nx - 1, ny - 1, pieces))] * 2
        + [dma((nx - 1, pieces))] * 2
        + [dma((nx - 1, ny - 1, pieces))] * 2
        + [dma((nx - 1, ny, nw, pieces))] * 2
        + [dma((pieces,))] * 2,
        compiler_params=pltpu.CompilerParams(
            collective_id=1, has_side_effects=True, vmem_limit_bytes=24 * 2**20
        ),
        name="gather_tiles",
    )(mine, tile_row.reshape(1, total), tile_column.reshape(1, total), features, grad_out)


def reduce_kernel(
    place,
    pieces,
    q,
    terms,
    out,
    own,
    mail,
    sc,
    rc,
    sx,
    rx,
    sy,
    ry,
    sz,
    rz,
    done,
    own_sem,
    mail_sem,
    cs,
    cr,
    xs,
    xr,
    ys,
    yr,
    zs,
    zr,
    keep_sem,
    azs,
    azr,
    ays,
    ayr,
):
    me = place.locate()
    nx, ny, nz = me.nx, me.ny, me.nz
    other = me.at(c=1 - me.c)
    xp, yp, zp = me.x_peers(), me.y_peers(), me.z_peers()
    meet([other] + xp + yp + zp)
    started = []

    def go(copy):
        copy.start()
        started.append(copy)

    def wide(ref):
        return ref[...].astype(jnp.float32)

    def core_copy(p):
        return remote(sc.at[p], rc.at[p], cs.at[p], cr.at[p], other)

    def own_copy(p):
        return pltpu.make_async_copy(terms.at[me.c, p], own.at[p], own_sem.at[p])

    def mail_copy(p):
        return pltpu.make_async_copy(terms.at[1 - me.c, p], mail.at[p], mail_sem.at[p])

    def x_copy(p, k):
        return remote(sx.at[p, k - 1], rx.at[p, k - 1], xs.at[p, k - 1], xr.at[p, k - 1], xp[k - 1])

    def y_copy(p, j):
        return remote(sy.at[p, j - 1], ry.at[p, j - 1], ys.at[p, j - 1], yr.at[p, j - 1], yp[j - 1])

    def z_copy(p, m):
        return remote(sz.at[p, m - 1], rz.at[p, m - 1], zs.at[p, m - 1], zr.at[p, m - 1], zp[m - 1])

    def spread_z(p, m, z):
        return remote(
            done.at[p], out.at[p, me.y, z], azs.at[p, m - 1], azr.at[p, m - 1], zp[m - 1]
        )

    def spread_y(p, j, m, src, y, z):
        return remote(
            src, out.at[p, y, z], ays.at[p, j - 1, m], ayr.at[p, j - 1, m], yp[j - 1]
        )

    def keep_copy(p):
        return pltpu.make_async_copy(done.at[p], out.at[p, me.y, me.z], keep_sem.at[p])

    def fetch(p):
        if p < pieces:
            mail_copy(p).start()
            own_copy(p).start()

    def post(p):
        if p < pieces:
            mail_copy(p).wait()

            def body(n, carry):
                for x in range(nx):
                    sc[p, x, n] = mail[p, x, n].astype(jnp.bfloat16)
                return carry

            lax.fori_loop(0, ny * nz * q, body, 0)
            go(core_copy(p))

    def over_x(p):
        own_copy(p).wait()
        core_copy(p).wait_recv()
        for k in range(1, nx):
            x = me.step_x(k)

            def body(n, carry):
                total = wide(own.at[p, x, n]) + wide(rc.at[p, x, n])
                sx[p, k - 1, n] = total.astype(jnp.bfloat16)
                return carry

            lax.fori_loop(0, ny * nz * q, body, 0)
            go(x_copy(p, k))
        post(p + WINDOW)
        fetch(p + WINDOW + 1)

    def up_to_x(p, n):
        total = wide(own.at[p, me.x, n]) + wide(rc.at[p, me.x, n])
        for k in range(1, nx):
            total = total + wide(rx.at[p, k - 1, n])
        return total

    def up_to_y(p, n):
        total = up_to_x(p, me.y * (nz * q) + n)
        for j in range(1, ny):
            total = total + wide(ry.at[p, j - 1, n])
        return total

    def over_y(p):
        for k in range(1, nx):
            x_copy(p, k).wait_recv()
        for j in range(1, ny):
            first = me.step_y(j) * (nz * q)

            def body(n, carry):
                sy[p, j - 1, n] = up_to_x(p, first + n).astype(jnp.bfloat16)
                return carry

            lax.fori_loop(0, nz * q, body, 0)
            go(y_copy(p, j))

    def over_z(p):
        for j in range(1, ny):
            y_copy(p, j).wait_recv()
        for m in range(1, nz):
            first = me.step_z(m) * q

            def body(i, carry):
                sz[p, m - 1, i] = up_to_y(p, first + i).astype(jnp.bfloat16)
                return carry

            lax.fori_loop(0, q, body, 0)
            go(z_copy(p, m))

    def finish(p):
        for m in range(1, nz):
            z_copy(p, m).wait_recv()

        def body(i, carry):
            total = up_to_y(p, me.z * q + i)
            for m in range(1, nz):
                total = total + wide(rz.at[p, m - 1, i])
            scale = lax.rsqrt(jnp.mean(total * total, keepdims=True) + 1e-06)
            done[p, i] = (total * scale).astype(jnp.bfloat16)
            return carry

        lax.fori_loop(0, q, body, 0)
        for m in range(1, nz):
            go(spread_z(p, m, me.z))
        for j in range(1, ny):
            go(spread_y(p, j, 0, done.at[p], me.y, me.z))
        keep_copy(p).start()

    def pass_on(p):
        for m in range(1, nz):
            z = me.step_z(-m)
            spread_z(p, m, z).wait_recv()
            for j in range(1, ny):
                go(spread_y(p, j, m, out.at[p, me.y, z], me.y, z))

    def collect(p):
        for j in range(1, ny):
            y = me.step_y(-j)
            for m in range(nz):
                z = me.step_z(-m)
                spread_y(p, j, m, done.at[p], y, z).wait_recv()

    for p in range(WINDOW + 1):
        fetch(p)
    for p in range(WINDOW):
        post(p)
    stages = [over_x, over_y, over_z, finish, pass_on, collect]
    lags = [0] + list(range(2, len(stages) + 1))
    for t in range(pieces + lags[-1]):
        for lag, stage in zip(lags, stages):
            if 0 <= t - lag < pieces:
                stage(t - lag)
    for p in range(pieces):
        keep_copy(p).wait()
    for copy in started:
        copy.wait_send()


def reduce_terms(terms, place, pieces, q):
    side = terms.shape[-1]
    nx, ny, nz = place.nx, place.ny, place.nz
    n = ny * nz * q
    dma = pltpu.SemaphoreType.DMA

    def room(*lead, dtype=jnp.bfloat16):
        return pltpu.VMEM((pieces,) + lead + (side, side), dtype)

    return pl.pallas_call(
        functools.partial(reduce_kernel, place, pieces, q),
        in_specs=[pl.BlockSpec(memory_space=pl.ANY)],
        out_specs=pl.BlockSpec(memory_space=pltpu.VMEM),
        out_shape=jax.ShapeDtypeStruct((pieces, ny, nz, q, side, side), jnp.bfloat16),
        scratch_shapes=[
            room(nx, n, dtype=jnp.float32),
            room(nx, n, dtype=jnp.float32),
            room(nx, n),
            room(nx, n),
            room(nx - 1, n),
            room(nx - 1, n),
            room(ny - 1, nz * q),
            room(ny - 1, nz * q),
            room(nz - 1, q),
            room(nz - 1, q),
            room(q),
            dma((pieces,)),
            dma((pieces,)),
            dma((pieces,)),
            dma((pieces,)),
            dma((pieces, nx - 1)),
            dma((pieces, nx - 1)),
            dma((pieces, ny - 1)),
            dma((pieces, ny - 1)),
            dma((pieces, nz - 1)),
            dma((pieces, nz - 1)),
            dma((pieces,)),
            dma((pieces, nz - 1)),
            dma((pieces, nz - 1)),
            dma((pieces, ny - 1, nz)),
            dma((pieces, ny - 1, nz)),
        ],
        compiler_params=pltpu.CompilerParams(
            collective_id=2, has_side_effects=True, vmem_limit_bytes=48 * 2**20
        ),
        name="reduce_terms",
    )(terms)


def on_device(n_dp, n_fsdp, features, grad_out, weight_tiles, tile_row, tile_column):
    tiles_here, side, _ = weight_tiles.shape
    nblocks = features.shape[1] // side
    place = Place(n_dp, n_fsdp)
    nx, n = place.nx, place.ny * place.nz
    pieces = max(count for count in (1, 2, 4, 8) if tiles_here % (n * count) == 0)
    n = tiles_here // pieces
    whole, blocks, tiles, places, features, grad_out = gather_tiles(
        weight_tiles, tile_row, tile_column, features, grad_out, nblocks, n, place
    )
    grad_features, partial = layer(features, grad_out, whole, blocks, tiles, places)
    terms = partial.reshape(2, pieces, nx, n, side, side)
    tile_update = reduce_terms(terms, place, pieces, n // (place.ny * place.nz))
    return (grad_features, tile_update.reshape(tiles_here, side, side).astype(jnp.float32))


def solution(mesh):
    return jax.shard_map(
        functools.partial(on_device, mesh.shape["dp"], mesh.shape["fsdp"]),
        mesh=mesh,
        in_specs=(
            P(("dp", "fsdp"), None),
            P(("dp", "fsdp"), None),
            P("fsdp", None, None),
            P(),
            P(),
        ),
        out_specs=(P(("dp", "fsdp"), None), P("fsdp", None, None)),
        check_vma=False,
    )
```
